256 devices in a mesh: lat: 8 (over x_hi, y), lon: 32 (over z, x_lo, core).
Axes of the slice: x: 4 (x_hi: 2, x_lo: 2; x = x_hi * 2 + x_lo), y: 4, z: 8, core: 2. Of those that a mesh axis runs over, the one named last changes fastest.
Arguments:
- background: bfloat16 [8, 32, 512, 1024], P('lat', 'lon'), may hold values from -6 to 6
- conv_pert: bfloat16 [8, 32, 128, 512], P('lat', 'lon'), may hold values from -6 to 6
- conv_misfit: bfloat16 [8, 32, 128], P('lat', 'lon'), may hold values from -6 to 6
- conv_column: int32 [8, 32, 128], P('lat', 'lon'), may hold values from 0 to 255
- sat_pert: bfloat16 [8, 512, 32, 512], P('lat', 'lon'), may hold values from -6 to 6
- sat_misfit: bfloat16 [8, 512, 32], P('lat', 'lon'), may hold values from -6 to 6
- sat_rows: int32 [8, 512], P('lat', 'lon'), may hold values from 1 to 32
- sat_targets: int32 [8, 512, 2], P('lat', 'lon'), may hold values from 0 to 31, all different within a row; in each aligned block of 16 rows (0 to 15, 16 to 31, ..., all dimensions but the last counted through in order) at most 2 rows name the same one
Outputs:
- analysis: float32 [8, 32, 512, 1024], P('lat', 'lon')
The draws below stay inside these ranges and needn't reach their ends.
Inputs may be any that keep to these rules, and one draw needn't show every extreme that they name: `sat_targets`: each tile names 2 different blocks. The tiles of one device name one block at most 2 times in all, and some device names some block exactly 2 times.
All inputs are finite; a program needn't handle non-finite values.
Results may differ from the reference program's by a relative error of at most 0.0073.
Values may be sent and summed in bfloat16 or wider, within the bound.
No kernel may reach another device: no remote copies, remote signals or barrier semaphores. Data moves between devices by JAX's collectives and lax.ppermute only.
A program may use at most 128 MiB of HBM per device.

```python
import math
import jax
import jax.numpy as jnp
import numpy as np
from jax import lax

K = 512
BLK = 16
CONV = 128
TILES_DEV = 16
TILE_OBS = 32
LOC = 2
NS_ITERS = 3
COLS = 256
CELLS = 1024
TILES = 512
CAP = 2
N_LAT = 8
N_LON = 32


def draw_background(key, part):
    key = jax.random.fold_in(key, 3)
    values = jax.random.normal(key, (N_LAT, N_LON, K, CELLS), jnp.float32)
    return jnp.clip(values, -6.0, 6.0).astype(jnp.bfloat16)


def draw_conv_pert(key, part):
    key = jax.random.fold_in(key, 5)
    values = jax.random.normal(key, (N_LAT, N_LON, CONV, K), jnp.float32)
    return jnp.clip(values, -6.0, 6.0).astype(jnp.bfloat16)


def draw_sat_pert(key, part):
    key = jax.random.fold_in(key, 7)
    values = jax.random.normal(key, (N_LAT, TILES, TILE_OBS, K), jnp.float32)
    return jnp.clip(values, -6.0, 6.0).astype(jnp.bfloat16)


def touch_ends(array, own_key, least, top_value):
    place = [jax.random.randint(jax.random.fold_in(own_key, axis), (), 0, length) for axis, length in enumerate(array.shape)]
    longest = array.shape.index(max(array.shape))
    next_to = place[:longest] + [(place[longest] + 1) % array.shape[longest]] + place[longest + 1:]
    return array.at[tuple(place)].set(least).at[tuple(next_to)].set(top_value)


def block_levels(stream_key, dims, split, smallest, high):
    level, own = 1.0, jax.random.fold_in(stream_key, 6)
    for axis_at, shards_of in split:
        heights = jnp.exp(jax.random.uniform(jax.random.fold_in(own, axis_at), (shards_of,), jnp.float32, smallest / len(split), high / len(split)))
        level = level * jnp.repeat(heights, dims[axis_at] // shards_of).reshape([-1 if axis == axis_at else 1 for axis in range(len(dims))])
    return level


def deal_out(stream_key, own, number, rows, count, top, limit, lean):
    sequence = jax.random.permutation(stream_key, count)
    heavy_load, common = shares(count, rows * top, limit, lean, True), shares(count, rows * top, limit, lean, False)
    places = jnp.arange(count)

    def named(sizes, rotation):
        used = int((sizes > 0).sum())
        fixed = max(1, used // 4)
        moved = fixed + (places - fixed + rotation * (used - fixed)) % max(1, count - fixed)
        return jnp.zeros((count,), jnp.int32).at[sequence[jnp.where(places < fixed, places, moved)]].set(jnp.asarray(sizes, jnp.int32))

    sizes = jnp.where(number % 4 == 0, named(heavy_load, number // 4), named(common, number - number // 4 - 1))
    mixed = jax.random.permutation(jax.random.fold_in(own, 3), count)
    source_of, sink = mixed[0:count // 2 * 2:2], mixed[1:count // 2 * 2:2]
    slack = jnp.minimum(sizes[source_of] - 1, limit - sizes[sink]) // 2
    slack = jnp.where((source_of == sequence[0]) | (sink == sequence[0]) | (sizes[sink] == 0), 0, jnp.maximum(slack, 0))
    moved = jax.random.randint(jax.random.fold_in(own, 4), (count // 2,), 0, 1 << 20) % (slack + 1)
    sizes = sizes.at[source_of].add(-moved).at[sink].add(moved)
    items = jnp.searchsorted(jnp.cumsum(sizes), jnp.arange(rows * top), side="right").astype(jnp.int32)
    grid = items.reshape(top, rows).T
    grid = grid[jax.random.permutation(jax.random.fold_in(own, 1), rows)]
    rotation = jax.random.randint(jax.random.fold_in(own, 2), (rows, 1), 0, top)
    return jnp.take_along_axis(grid, (jnp.arange(top)[None, :] + rotation) % top, axis=1)


def shares(amount, total, limit, lean, full):
    weights = [(1 << 20) // math.isqrt(standing ** lean) + 1 for standing in range(1, amount + 1)]
    largest = limit if full else min(limit, max(-(-total // amount), total * weights[0] // sum(weights)))
    least = 1 if total - largest >= amount - 1 else 0
    holding, spare = [largest] + [least] * (amount - 1), total - largest - least * (amount - 1)
    while spare > 0:
        movable = [i for i in range(1, amount) if holding[i] < largest] or [i for i in range(1, amount) if holding[i] < limit]
        pool, budget = sum([weights[i] for i in movable]), spare
        for i in movable:
            addition = min(limit - holding[i], max(1, budget * weights[i] // pool), spare)
            holding[i] = holding[i] + addition
            spare = spare - addition
    return np.array(holding)


def normal_values(own_key, shape, scale, reach, split=(), kind=jnp.bfloat16):
    values = scale * jax.random.normal(own_key, shape, jnp.float32)
    if split:
        values = values * block_levels(own_key, shape, split, -0.22, 0.18)
    return jnp.clip(values, -reach, reach).astype(kind)


def setup_inputs(seed: int = 0) -> dict:
    arg_keys = jax.random.split(jax.random.key(seed), 9)
    background = draw_background(jax.random.fold_in(arg_keys[8], 71), 0)
    conv_pert = draw_conv_pert(jax.random.fold_in(arg_keys[8], 71), 0)
    conv_misfit = normal_values(arg_keys[2], (N_LAT, N_LON, CONV), 1.0, 6.0, ((0, 8), (1, 32)))
    conv_column = touch_ends(jax.random.randint(arg_keys[3], (N_LAT, N_LON, CONV), 0, COLS), jax.random.fold_in(arg_keys[3], 1), 0, COLS - 1).astype(jnp.int32)
    sat_pert = draw_sat_pert(jax.random.fold_in(arg_keys[8], 71), 0)
    sat_misfit = normal_values(arg_keys[5], (N_LAT, TILES, TILE_OBS), 1.0, 6.0, ((0, 8), (1, 32)))
    sat_rows = touch_ends(jax.random.randint(arg_keys[6], (N_LAT, TILES), 1, TILE_OBS + 1), jax.random.fold_in(arg_keys[6], 1), 1, TILE_OBS).astype(jnp.int32)
    sat_targets_keys = jax.random.split(jax.random.fold_in(arg_keys[7], 1), N_LAT * TILES // TILES_DEV)
    sat_targets_turns = jax.random.permutation(jax.random.fold_in(arg_keys[7], 3), N_LAT * TILES // TILES_DEV)
    sat_targets = jax.vmap(lambda own, number: deal_out(jax.random.fold_in(arg_keys[7], 2), own, number, TILES_DEV, N_LON, LOC, CAP, 2))(sat_targets_keys, sat_targets_turns).reshape((N_LAT, TILES, LOC))
    return {"background": background, "conv_pert": conv_pert, "conv_misfit": conv_misfit, "conv_column": conv_column, "sat_pert": sat_pert, "sat_misfit": sat_misfit, "sat_rows": sat_rows, "sat_targets": sat_targets}


def local_weight(column, lat_shift, lon_shift):
    lat_place = BLK * lat_shift + (column // BLK).astype(jnp.float32) + 0.5 - 0.5 * BLK
    lon_place = BLK * lon_shift + (column % BLK).astype(jnp.float32) + 0.5 - 0.5 * BLK
    return jnp.exp(-(lat_place * lat_place + lon_place * lon_place) / (2.0 * BLK * BLK))

def analyse(gram_sum, drive_sum, ensemble):
    members = ensemble.shape[0]
    highest = lax.Precision.HIGHEST
    identity = jnp.eye(members, dtype=jnp.float32)
    system = (members - 1.0) * identity + gram_sum
    scale = jnp.sqrt(jnp.sum(system * system))
    iterate = system / scale
    inverse_root = identity
    for sweep_index in range(NS_ITERS):
        middle = 1.5 * identity - 0.5 * jnp.dot(inverse_root, iterate, precision=highest)
        iterate = jnp.dot(iterate, middle, precision=highest)
        inverse_root = jnp.dot(middle, inverse_root, precision=highest)
    covariance = jnp.dot(inverse_root, inverse_root, precision=highest) / scale
    mean_weight = jnp.dot(covariance, drive_sum, precision=highest)
    transform = (jnp.sqrt((members - 1.0) / scale) * inverse_root + mean_weight[:, None]).astype(jnp.bfloat16)
    state_mean = lax.optimization_barrier(jnp.mean(ensemble.astype(jnp.float32), axis=0))
    anomaly = (ensemble.astype(jnp.float32) - state_mean).astype(jnp.bfloat16)
    return state_mean + lax.dot_general(transform, anomaly, (((0,), (0,)), ((), ())), preferred_element_type=jnp.float32)

def shift_blocks(values, lat_shift, lon_shift):
    rolled = jnp.roll(values, -lon_shift, axis=1)
    widths = [(1, 1)] + [(0, 0)] * (values.ndim - 1)
    padded = jnp.pad(rolled, widths)
    return padded[1 + lat_shift:1 + lat_shift + values.shape[0]]

def reference(background, conv_pert, conv_misfit, conv_column, sat_pert, sat_misfit, sat_rows, sat_targets):
    tile_total = TILES_DEV * N_LON
    entry_weight = 0.5 ** jnp.arange(LOC).astype(jnp.float32)
    obs_index = jnp.arange(TILE_OBS).astype(jnp.int32)

    def add_tile(tile_number, totals):
        gram_all, drive_all = totals
        band_index = tile_number // tile_total
        tile_slot = tile_number % tile_total
        spread = sat_pert[band_index, tile_slot]
        misfit = sat_misfit[band_index, tile_slot]
        live = obs_index < sat_rows[band_index, tile_slot]
        for list_slot in range(LOC):
            target = sat_targets[band_index, tile_slot, list_slot]
            keep_rows = jnp.where(live, entry_weight[list_slot], 0.0)
            scaled = (keep_rows[:, None] * spread).astype(jnp.bfloat16)
            gram_all = gram_all.at[band_index, target].add(jnp.dot(scaled.T, spread, preferred_element_type=jnp.float32))
            drive_all = drive_all.at[band_index, target].add(jnp.dot(misfit, scaled, preferred_element_type=jnp.float32))
        return (gram_all, drive_all)
    gram_all = jnp.zeros((N_LAT, N_LON, K, K), jnp.float32)
    drive_all = jnp.zeros((N_LAT, N_LON, K), jnp.float32)
    gram_all, drive_all = lax.fori_loop(0, N_LAT * tile_total, add_tile, (gram_all, drive_all))
    for lat_shift in (-1, 0, 1):
        for lon_shift in (-1, 0, 1):
            spread = shift_blocks(conv_pert, lat_shift, lon_shift)
            misfit = shift_blocks(conv_misfit, lat_shift, lon_shift)
            column = shift_blocks(conv_column, lat_shift, lon_shift)
            weight = local_weight(column, lat_shift, lon_shift)
            scaled = (weight[..., None] * spread).astype(jnp.bfloat16)
            gram_all = gram_all + jnp.einsum('abok,abol->abkl', scaled.astype(jnp.float32), spread.astype(jnp.float32))
            drive_all = drive_all + jnp.einsum('abok,abo->abk', scaled.astype(jnp.float32), misfit.astype(jnp.float32))
    flat = (gram_all.reshape(-1, K, K), drive_all.reshape(-1, K), background.reshape(-1, K, CELLS))
    result = lax.map(lambda block_items: analyse(*block_items), flat)
    return result.reshape(N_LAT, N_LON, K, CELLS)
```

```python
import functools

import jax
import jax.numpy as jnp
from jax import lax
from jax.experimental import pallas as pl
from jax.experimental.pallas import tpu as pltpu
from jax.sharding import PartitionSpec as P

BLK = 16
LOC = 2
F32 = jnp.float32
BF16 = jnp.bfloat16
PAD = 16
VMEM = pltpu.VMEM
SMEM = pltpu.SMEM
LIMIT = 48 * 1024 * 1024


def call(body, outs, in_spaces, scratch=(), flops=0, moved=0):
    return pl.pallas_call(
        body,
        out_shape=outs,
        in_specs=[pl.BlockSpec(memory_space=space) for space in in_spaces],
        out_specs=jax.tree.map(lambda _: pl.BlockSpec(memory_space=VMEM), outs),
        scratch_shapes=list(scratch),
        compiler_params=pltpu.CompilerParams(vmem_limit_bytes=LIMIT),
        cost_estimate=pl.CostEstimate(flops=flops, bytes_accessed=moved, transcendentals=0),
    )


def transposed_dot(left, right):
    return lax.dot_general(left, right, (((0,), (0,)), ((), ())), preferred_element_type=F32)


def dot(left, right):
    return jnp.dot(left, right, preferred_element_type=F32)


def background_body(ensemble_ref, anomaly_ref, mean_ref):
    values = ensemble_ref[...].astype(F32)
    mean = jnp.mean(values, axis=0, keepdims=True)
    mean_ref[...] = mean
    anomaly_ref[...] = (values - mean).astype(BF16)


def route_body(pert_ref, misfit_ref, rows_ref, targets_ref, slots_ref, drive_ref, entry_ref, count_ref):
    tiles, obs, members = pert_ref.shape
    blocks = slots_ref.shape[0]

    def clear(block, _):
        count_ref[block] = 0
        entry_ref[2 * block] = -1
        entry_ref[2 * block + 1] = -1
        return 0

    lax.fori_loop(0, blocks, clear, 0)
    for tile in range(tiles):
        for k in range(LOC):
            block = targets_ref[LOC * tile + k]
            used = count_ref[block]
            entry_ref[2 * block + used] = LOC * tile + k
            count_ref[block] = used + 1
    row = lax.broadcasted_iota(jnp.int32, (obs, members), 0)

    def fill(slot, _):
        entry = entry_ref[slot]
        safe = jnp.maximum(entry, 0)
        tile = safe // LOC
        live = jnp.where(entry >= 0, rows_ref[tile], 0)
        factor = jnp.where(safe % LOC == 0, 1.0, 0.5**0.5).astype(F32)
        values = pert_ref[tile].astype(F32) * factor
        start = pl.multiple_of((slot % 2) * obs, obs)
        slots_ref[slot // 2, pl.ds(start, obs), :] = jnp.where(row < live, values, 0.0).astype(BF16)
        return 0

    lax.fori_loop(0, 2 * blocks, fill, 0)
    total = tiles * obs
    lane = lax.broadcasted_iota(jnp.int32, (1, total), 1)
    own_tile = lane // obs
    live = jnp.zeros((1, total), jnp.int32)
    named = [jnp.zeros((1, total), jnp.int32) for _ in range(LOC)]
    for tile in range(tiles):
        here = own_tile == tile
        live = jnp.where(here, rows_ref[tile], live)
        for k in range(LOC):
            named[k] = jnp.where(here, targets_ref[LOC * tile + k], named[k])
    repeat = (
        lax.broadcasted_iota(jnp.int32, (obs, total), 1) % obs
        == lax.broadcasted_iota(jnp.int32, (obs, total), 0)
    )
    spread = dot(misfit_ref[...], jnp.where(repeat, 1.0, 0.0).astype(BF16))
    pick = lax.broadcasted_iota(jnp.int32, (tiles, total), 1) // obs == lax.broadcasted_iota(
        jnp.int32, (tiles, total), 0
    )
    misfit = jnp.sum(jnp.where(pick, spread, 0.0), axis=0, keepdims=True)
    misfit = jnp.where(lane % obs < live, misfit, 0.0)
    block = lax.broadcasted_iota(jnp.int32, (blocks, total), 0)
    weight = jnp.zeros((blocks, total), F32)
    for k in range(LOC):
        weight = weight + jnp.where(block == named[k], 0.5**k, 0.0)
    drive_ref[...] = dot((weight * misfit).astype(BF16), pert_ref[...].reshape(total, members))


def conv_body(middle_ref, south_ref, north_ref, gram_ref, drive_ref, scaled_ref, spread_ref):
    conv, members = middle_ref.shape[1] - PAD, middle_ref.shape[2]
    eye = lax.broadcasted_iota(jnp.int32, (conv, conv), 0) == lax.broadcasted_iota(
        jnp.int32, (conv, conv), 1
    )
    drive = jnp.zeros((8, members), F32)
    for a, ref in ((-1, south_ref), (0, middle_ref), (1, north_ref)):
        for b in (-1, 0, 1):
            misfit = ref[b + 1, conv : conv + 1, 0:conv]
            column = ref[b + 1, conv : conv + 1, conv : 2 * conv].astype(F32)
            lat_cell = jnp.floor(column * (1.0 / BLK))
            lon_cell = column - BLK * lat_cell
            lat_place = BLK * a + lat_cell + 0.5 - 0.5 * BLK
            lon_place = BLK * b + lon_cell + 0.5 - 0.5 * BLK
            weight = jnp.exp(-(lat_place * lat_place + lon_place * lon_place) / (2.0 * BLK * BLK))
            weight = jnp.sum(jnp.where(eye, weight, 0.0), axis=1, keepdims=True)
            rows = ref[b + 1, 0:conv, :]
            scaled = (weight * rows.astype(F32)).astype(BF16)
            at = ((a + 1) * 3 + b + 1) * conv
            scaled_ref[at : at + conv, :] = scaled
            spread_ref[at : at + conv, :] = rows
            drive = drive + dot(jnp.broadcast_to(misfit, (8, conv)), scaled)
    drive_ref[...] = drive[0:1]
    gram_ref[...] = transposed_dot(scaled_ref[...], spread_ref[...])


def root_and_apply(gram, drive, mean_ref, anomaly_ref, out_ref):
    members = gram.shape[0]
    eye = lax.broadcasted_iota(jnp.int32, gram.shape, 0) == lax.broadcasted_iota(
        jnp.int32, gram.shape, 1
    )
    system = gram + jnp.where(eye, members - 1.0, 0.0)
    square = jnp.sum(jnp.sum(system * system, axis=0, keepdims=True), axis=1, keepdims=True)
    inverse_scale = lax.rsqrt(square)
    power1 = system * inverse_scale
    half1 = power1.astype(BF16)
    power2 = dot(half1, half1)
    half2 = power2.astype(BF16)
    power3 = dot(half1, half2)
    power4 = dot(half2, half2)
    product = 2.25 * power1 - 1.5 * power2 + 0.25 * power3
    excess = -0.75 * (power1 + product) + 0.25 * (2.25 * power2 - 1.5 * power3 + 0.25 * power4)
    half_excess = excess.astype(BF16)
    lifted = 4.5 * excess + dot(half_excess, half_excess)
    product = 5.0625 * power1 + dot(half1, lifted.astype(BF16))
    inverse_root = 1.5 * excess - 1.125 * product - 0.5 * dot(product.astype(BF16), half_excess)
    inverse_root = inverse_root + jnp.where(eye, 3.375, 0.0)
    first = jnp.sum(inverse_root * drive, axis=1, keepdims=True)
    weight = jnp.sum(inverse_root * first, axis=0, keepdims=True) * inverse_scale
    transform = (jnp.sqrt((members - 1.0) * inverse_scale) * inverse_root + weight).astype(BF16)
    out_ref[...] = mean_ref[...] + dot(transform, anomaly_ref[...])


def final_body(rows_ref, conv_ref, drive1_ref, drive2_ref, mean_ref, anomaly_ref, out_ref):
    rows = rows_ref[...]
    gram = conv_ref[...] + transposed_dot(rows, rows)
    root_and_apply(gram, drive1_ref[...] + drive2_ref[...], mean_ref, anomaly_ref, out_ref)


def shards(
    background, conv_pert, conv_misfit, conv_column, sat_pert, sat_misfit, sat_rows, sat_targets
):
    members, cells = background.shape[2:]
    conv = conv_pert.shape[2]
    tiles, obs = sat_pert.shape[1:3]
    blocks, bands = lax.axis_size("lon"), lax.axis_size("lat")
    shape = jax.ShapeDtypeStruct

    extra = jnp.concatenate([conv_misfit[0], conv_column[0].astype(BF16)], axis=1)
    extra = jnp.pad(extra, ((0, PAD - 1), (0, members - 2 * conv)))
    own = jnp.concatenate([conv_pert[0, 0], extra], axis=0)
    east = [(i, (i + 1) % blocks) for i in range(blocks)]
    west = [(target, source) for source, target in east]
    low = lax.ppermute(own, "lon", east)
    high = lax.ppermute(own, "lon", west)

    slots, drive = call(
        route_body,
        (shape((blocks, 2 * obs, members), BF16), shape((blocks, members), F32)),
        [VMEM, VMEM, SMEM, SMEM],
        [pltpu.SMEM((2 * blocks,), jnp.int32), pltpu.SMEM((blocks,), jnp.int32)],
    )(sat_pert[0], sat_misfit[0], sat_rows[0], sat_targets.reshape(-1))

    middle = jnp.stack([low, own, high])
    up = [(i, i + 1) for i in range(bands - 1)]
    down = [(target, source) for source, target in up]
    south = lax.ppermute(middle, "lat", up)
    north = lax.ppermute(middle, "lat", down)
    drive_sat = lax.psum_scatter(drive, "lon", scatter_dimension=0, tiled=True)
    rows = lax.all_to_all(slots, "lon", 0, 0, tiled=True).reshape(blocks * 2 * obs, members)

    anomaly, mean = call(
        background_body, (shape((members, cells), BF16), shape((1, cells), F32)), [VMEM]
    )(background[0, 0])
    gram_conv, drive_conv = call(
        conv_body,
        (shape((members, members), F32), shape((1, members), F32)),
        [VMEM] * 3,
        [pltpu.VMEM((9 * conv, members), BF16), pltpu.VMEM((9 * conv, members), BF16)],
    )(middle, south, north)
    result = call(final_body, shape((members, cells), F32), [VMEM] * 6)(
        rows, gram_conv, drive_conv, drive_sat, mean, anomaly
    )
    return result[None, None]


def solution(mesh):
    placed = (
        P("lat", "lon", None, None),
        P("lat", "lon", None, None),
        P("lat", "lon", None),
        P("lat", "lon", None),
        P("lat", "lon", None, None),
        P("lat", "lon", None),
        P("lat", "lon"),
        P("lat", "lon", None),
    )
    return jax.shard_map(
        shards, mesh=mesh, in_specs=placed, out_specs=P("lat", "lon", None, None), check_vma=False
    )
```

```python
import functools

import jax
import jax.numpy as jnp
from jax import lax
from jax.experimental import pallas as pl
from jax.experimental.pallas import tpu as pltpu
from jax.sharding import PartitionSpec as P

BLK = 16
LOC = 2
F32 = jnp.float32
BF16 = jnp.bfloat16
PAD = 16
LANES = 128
VMEM = pltpu.VMEM
SMEM = pltpu.SMEM
LIMIT = 48 * 1024 * 1024


def call(body, outs, in_spaces, scratch=(), flops=0, moved=0):
    return pl.pallas_call(
        body,
        out_shape=outs,
        in_specs=[pl.BlockSpec(memory_space=space) for space in in_spaces],
        out_specs=jax.tree.map(lambda _: pl.BlockSpec(memory_space=VMEM), outs),
        scratch_shapes=list(scratch),
        compiler_params=pltpu.CompilerParams(vmem_limit_bytes=LIMIT),
        cost_estimate=pl.CostEstimate(flops=flops, bytes_accessed=moved, transcendentals=0),
    )


def transposed_dot(left, right):
    return lax.dot_general(left, right, (((0,), (0,)), ((), ())), preferred_element_type=F32)


def dot(left, right):
    return jnp.dot(left, right, preferred_element_type=F32)


def background_body(ensemble_ref, anomaly_ref, mean_ref):
    values = ensemble_ref[...].astype(F32)
    mean = jnp.mean(values, axis=0, keepdims=True)
    mean_ref[...] = mean
    anomaly_ref[...] = (values - mean).astype(BF16)


def route_body(pert_ref, misfit_ref, rows_ref, targets_ref, slots_ref, entry_ref, count_ref):
    tiles, obs, members = pert_ref.shape
    blocks = slots_ref.shape[0]

    def clear(block, _):
        count_ref[block] = 0
        entry_ref[2 * block] = -1
        entry_ref[2 * block + 1] = -1
        return 0

    lax.fori_loop(0, blocks, clear, 0)
    for tile in range(tiles):
        for k in range(LOC):
            block = targets_ref[LOC * tile + k]
            used = count_ref[block]
            entry_ref[2 * block + used] = LOC * tile + k
            count_ref[block] = used + 1
    row = lax.broadcasted_iota(jnp.int32, (obs, members), 0)

    def fill(slot, _):
        entry = entry_ref[slot]
        safe = jnp.maximum(entry, 0)
        tile = safe // LOC
        live = jnp.where(entry >= 0, rows_ref[tile], 0)
        factor = jnp.where(safe % LOC == 0, 1.0, 0.5**0.5).astype(F32)
        values = pert_ref[tile].astype(F32) * factor
        values = jnp.where(row < live, values, 0.0).astype(BF16)
        for part in range(members // LANES):
            start = pl.multiple_of(part * 2 * obs + (slot % 2) * obs, obs)
            slots_ref[slot // 2, pl.ds(start, obs), :] = values[:, part * LANES : (part + 1) * LANES]
        return 0

    lax.fori_loop(0, 2 * blocks, fill, 0)
    total = tiles * obs
    lane = lax.broadcasted_iota(jnp.int32, (1, total), 1)
    own_tile = lane // obs
    live = jnp.zeros((1, total), jnp.int32)
    named = [jnp.zeros((1, total), jnp.int32) for _ in range(LOC)]
    for tile in range(tiles):
        here = own_tile == tile
        live = jnp.where(here, rows_ref[tile], live)
        for k in range(LOC):
            named[k] = jnp.where(here, targets_ref[LOC * tile + k], named[k])
    repeat = (
        lax.broadcasted_iota(jnp.int32, (obs, total), 1) % obs
        == lax.broadcasted_iota(jnp.int32, (obs, total), 0)
    )
    spread = dot(misfit_ref[...], jnp.where(repeat, 1.0, 0.0).astype(BF16))
    pick = lax.broadcasted_iota(jnp.int32, (tiles, total), 1) // obs == lax.broadcasted_iota(
        jnp.int32, (tiles, total), 0
    )
    misfit = jnp.sum(jnp.where(pick, spread, 0.0), axis=0, keepdims=True)
    misfit = jnp.where(lane % obs < live, misfit, 0.0)
    block = lax.broadcasted_iota(jnp.int32, (blocks, total), 0)
    weight = jnp.zeros((blocks, total), F32)
    for k in range(LOC):
        weight = weight + jnp.where(block == named[k], 0.5**k, 0.0)
    drive = dot((weight * misfit).astype(BF16), pert_ref[...].reshape(total, members))
    upper = drive.astype(BF16).astype(F32)
    parts = []
    for piece in (upper, drive - upper):
        for part in range(members // LANES):
            parts.append(piece[:, None, part * LANES : (part + 1) * LANES])
    parts.append(jnp.zeros((blocks, PAD - len(parts), LANES), F32))
    slots_ref[:, members // LANES * 2 * obs :, :] = jnp.concatenate(parts, axis=1).astype(BF16)


def conv_body(middle_ref, south_ref, north_ref, gram_ref, drive_ref, scaled_ref, spread_ref):
    conv, members = middle_ref.shape[1] - PAD, middle_ref.shape[2]
    eye = lax.broadcasted_iota(jnp.int32, (conv, conv), 0) == lax.broadcasted_iota(
        jnp.int32, (conv, conv), 1
    )
    drive = jnp.zeros((8, members), F32)
    for a, ref in ((-1, south_ref), (0, middle_ref), (1, north_ref)):
        for b in (-1, 0, 1):
            misfit = ref[b + 1, conv : conv + 1, 0:conv]
            column = ref[b + 1, conv : conv + 1, conv : 2 * conv].astype(F32)
            lat_cell = jnp.floor(column * (1.0 / BLK))
            lon_cell = column - BLK * lat_cell
            lat_place = BLK * a + lat_cell + 0.5 - 0.5 * BLK
            lon_place = BLK * b + lon_cell + 0.5 - 0.5 * BLK
            weight = jnp.exp(-(lat_place * lat_place + lon_place * lon_place) / (2.0 * BLK * BLK))
            weight = jnp.sum(jnp.where(eye, weight, 0.0), axis=1, keepdims=True)
            rows = ref[b + 1, 0:conv, :]
            scaled = (weight * rows.astype(F32)).astype(BF16)
            at = ((a + 1) * 3 + b + 1) * conv
            scaled_ref[at : at + conv, :] = scaled
            spread_ref[at : at + conv, :] = rows
            drive = drive + dot(jnp.broadcast_to(misfit, (8, conv)), scaled)
    drive_ref[...] = drive[0:1]
    gram_ref[...] = transposed_dot(scaled_ref[...], spread_ref[...])


def root_and_apply(gram, drive, mean_ref, anomaly_ref, out_ref):
    members = gram.shape[0]
    eye = lax.broadcasted_iota(jnp.int32, gram.shape, 0) == lax.broadcasted_iota(
        jnp.int32, gram.shape, 1
    )
    system = gram + jnp.where(eye, members - 1.0, 0.0)
    square = jnp.sum(jnp.sum(system * system, axis=0, keepdims=True), axis=1, keepdims=True)
    inverse_scale = lax.rsqrt(square)
    power1 = system * inverse_scale
    half1 = power1.astype(BF16)
    power2 = dot(half1, half1)
    half2 = power2.astype(BF16)
    power3 = dot(half1, half2)
    power4 = dot(half2, half2)
    product = 2.25 * power1 - 1.5 * power2 + 0.25 * power3
    excess = -0.75 * (power1 + product) + 0.25 * (2.25 * power2 - 1.5 * power3 + 0.25 * power4)
    half_excess = excess.astype(BF16)
    lifted = 4.5 * excess + dot(half_excess, half_excess)
    product = 5.0625 * power1 + dot(half1, lifted.astype(BF16))
    inverse_root = 1.5 * excess - 1.125 * product - 0.5 * dot(product.astype(BF16), half_excess)
    inverse_root = inverse_root + jnp.where(eye, 3.375, 0.0)
    first = jnp.sum(inverse_root * drive, axis=1, keepdims=True)
    weight = jnp.sum(inverse_root * first, axis=0, keepdims=True) * inverse_scale
    transform = (jnp.sqrt((members - 1.0) * inverse_scale) * inverse_root + weight).astype(BF16)
    out_ref[...] = mean_ref[...] + dot(transform, anomaly_ref[...])


def final_body(slots_ref, conv_ref, drive_ref, mean_ref, anomaly_ref, out_ref, rows_ref):
    blocks, pieces = slots_ref.shape[0], out_ref.shape[0] // LANES
    count = (slots_ref.shape[1] - PAD) // pieces
    for part in range(pieces):
        rows_ref[:, part * LANES : (part + 1) * LANES] = slots_ref[
            :, part * count : (part + 1) * count, :
        ].reshape(blocks * count, LANES)
    rows = rows_ref[...]
    gram = conv_ref[...] + transposed_dot(rows, rows)
    extra = jnp.sum(slots_ref[:, pieces * count :, :].astype(F32), axis=0)
    extra = extra[0:pieces] + extra[pieces : 2 * pieces]
    extra = jnp.concatenate([extra[part : part + 1] for part in range(pieces)], axis=1)
    root_and_apply(gram, drive_ref[...] + extra, mean_ref, anomaly_ref, out_ref)


def shards(
    background, conv_pert, conv_misfit, conv_column, sat_pert, sat_misfit, sat_rows, sat_targets
):
    members, cells = background.shape[2:]
    conv = conv_pert.shape[2]
    tiles, obs = sat_pert.shape[1:3]
    blocks, bands = lax.axis_size("lon"), lax.axis_size("lat")
    shape = jax.ShapeDtypeStruct

    extra = jnp.concatenate([conv_misfit[0], conv_column[0].astype(BF16)], axis=1)
    extra = jnp.pad(extra, ((0, PAD - 1), (0, members - 2 * conv)))
    own = jnp.concatenate([conv_pert[0, 0], extra], axis=0)
    east = [(i, (i + 1) % blocks) for i in range(blocks)]
    west = [(target, source) for source, target in east]
    low = lax.ppermute(own, "lon", east)
    high = lax.ppermute(own, "lon", west)

    slots = call(
        route_body,
        shape((blocks, members // LANES * 2 * obs + PAD, LANES), BF16),
        [VMEM, VMEM, SMEM, SMEM],
        [pltpu.SMEM((2 * blocks,), jnp.int32), pltpu.SMEM((blocks,), jnp.int32)],
    )(sat_pert[0], sat_misfit[0], sat_rows[0], sat_targets.reshape(-1))

    middle = jnp.stack([low, own, high])
    up = [(i, i + 1) for i in range(bands - 1)]
    down = [(target, source) for source, target in up]
    south = lax.ppermute(middle, "lat", up)
    north = lax.ppermute(middle, "lat", down)
    slots = lax.all_to_all(slots, "lon", 0, 0, tiled=True)

    anomaly, mean = call(
        background_body, (shape((members, cells), BF16), shape((1, cells), F32)), [VMEM]
    )(background[0, 0])
    gram_conv, drive_conv = call(
        conv_body,
        (shape((members, members), F32), shape((1, members), F32)),
        [VMEM] * 3,
        [pltpu.VMEM((9 * conv, members), BF16), pltpu.VMEM((9 * conv, members), BF16)],
    )(middle, south, north)
    result = call(
        final_body,
        shape((members, cells), F32),
        [VMEM] * 5,
        [pltpu.VMEM((blocks * 2 * obs, members), BF16)],
    )(slots, gram_conv, drive_conv, mean, anomaly)
    return result[None, None]


def solution(mesh):
    placed = (
        P("lat", "lon", None, None),
        P("lat", "lon", None, None),
        P("lat", "lon", None),
        P("lat", "lon", None),
        P("lat", "lon", None, None),
        P("lat", "lon", None),
        P("lat", "lon"),
        P("lat", "lon", None),
    )
    return jax.shard_map(
        shards, mesh=mesh, in_specs=placed, out_specs=P("lat", "lon", None, None), check_vma=False
    )
```

```python
import functools

import jax
import jax.numpy as jnp
from jax import lax
from jax.experimental import pallas as pl
from jax.experimental.pallas import tpu as pltpu
from jax.sharding import PartitionSpec as P

BLK = 16
LOC = 2
F32 = jnp.float32
BF16 = jnp.bfloat16
PAD = 16
LANES = 128
VMEM = pltpu.VMEM
SMEM = pltpu.SMEM
LIMIT = 48 * 1024 * 1024


def call(body, outs, in_spaces, scratch=(), flops=0, moved=0):
    return pl.pallas_call(
        body,
        out_shape=outs,
        in_specs=[pl.BlockSpec(memory_space=space) for space in in_spaces],
        out_specs=jax.tree.map(lambda _: pl.BlockSpec(memory_space=VMEM), outs),
        scratch_shapes=list(scratch),
        compiler_params=pltpu.CompilerParams(vmem_limit_bytes=LIMIT),
        cost_estimate=pl.CostEstimate(flops=flops, bytes_accessed=moved, transcendentals=0),
    )


def transposed_dot(left, right):
    return lax.dot_general(left, right, (((0,), (0,)), ((), ())), preferred_element_type=F32)


def dot(left, right):
    return jnp.dot(left, right, preferred_element_type=F32)


def background_body(ensemble_ref, anomaly_ref, mean_ref):
    values = ensemble_ref[...].astype(F32)
    mean = jnp.mean(values, axis=0, keepdims=True)
    mean_ref[...] = mean
    anomaly_ref[...] = (values - mean).astype(BF16)


def route_body(pert_ref, misfit_ref, rows_ref, targets_ref, slots_ref, entry_ref, count_ref):
    tiles, obs, members = pert_ref.shape
    blocks = slots_ref.shape[0]

    def clear(block, _):
        count_ref[block] = 0
        entry_ref[2 * block] = -1
        entry_ref[2 * block + 1] = -1
        return 0

    lax.fori_loop(0, blocks, clear, 0)
    for tile in range(tiles):
        for k in range(LOC):
            block = targets_ref[LOC * tile + k]
            used = count_ref[block]
            entry_ref[2 * block + used] = LOC * tile + k
            count_ref[block] = used + 1
    row = lax.broadcasted_iota(jnp.int32, (obs, members), 0)

    def fill(slot, _):
        entry = entry_ref[slot]
        safe = jnp.maximum(entry, 0)
        tile = safe // LOC
        live = jnp.where(entry >= 0, rows_ref[tile], 0)
        factor = jnp.where(safe % LOC == 0, 1.0, 0.5**0.5).astype(F32)
        values = pert_ref[tile].astype(F32) * factor
        values = jnp.where(row < live, values, 0.0).astype(BF16)
        for part in range(members // LANES):
            start = pl.multiple_of(part * 2 * obs + (slot % 2) * obs, obs)
            slots_ref[slot // 2, pl.ds(start, obs), :] = values[:, part * LANES : (part + 1) * LANES]
        return 0

    lax.fori_loop(0, 2 * blocks, fill, 0)
    total = tiles * obs
    lane = lax.broadcasted_iota(jnp.int32, (1, total), 1)
    own_tile = lane // obs
    live = jnp.zeros((1, total), jnp.int32)
    named = [jnp.zeros((1, total), jnp.int32) for _ in range(LOC)]
    for tile in range(tiles):
        here = own_tile == tile
        live = jnp.where(here, rows_ref[tile], live)
        for k in range(LOC):
            named[k] = jnp.where(here, targets_ref[LOC * tile + k], named[k])
    repeat = (
        lax.broadcasted_iota(jnp.int32, (obs, total), 1) % obs
        == lax.broadcasted_iota(jnp.int32, (obs, total), 0)
    )
    spread = dot(misfit_ref[...], jnp.where(repeat, 1.0, 0.0).astype(BF16))
    pick = lax.broadcasted_iota(jnp.int32, (tiles, total), 1) // obs == lax.broadcasted_iota(
        jnp.int32, (tiles, total), 0
    )
    misfit = jnp.sum(jnp.where(pick, spread, 0.0), axis=0, keepdims=True)
    misfit = jnp.where(lane % obs < live, misfit, 0.0)
    block = lax.broadcasted_iota(jnp.int32, (blocks, total), 0)
    weight = jnp.zeros((blocks, total), F32)
    for k in range(LOC):
        weight = weight + jnp.where(block == named[k], 0.5**k, 0.0)
    drive = dot((weight * misfit).astype(BF16), pert_ref[...].reshape(total, members))
    upper = drive.astype(BF16).astype(F32)
    parts = []
    for piece in (upper, drive - upper):
        for part in range(members // LANES):
            parts.append(piece[:, None, part * LANES : (part + 1) * LANES])
    parts.append(jnp.zeros((blocks, PAD - len(parts), LANES), F32))
    slots_ref[:, members // LANES * 2 * obs :, :] = jnp.concatenate(parts, axis=1).astype(BF16)


def conv_body(middle_ref, south_ref, north_ref, gram_ref, drive_ref, scaled_ref, spread_ref):
    conv, members = middle_ref.shape[1] - PAD, middle_ref.shape[2]
    eye = lax.broadcasted_iota(jnp.int32, (conv, conv), 0) == lax.broadcasted_iota(
        jnp.int32, (conv, conv), 1
    )
    drive = jnp.zeros((8, members), F32)
    for a, ref in ((-1, south_ref), (0, middle_ref), (1, north_ref)):
        for b in (-1, 0, 1):
            misfit = ref[b + 1, conv : conv + 1, 0:conv]
            column = ref[b + 1, conv : conv + 1, conv : 2 * conv].astype(F32)
            lat_cell = jnp.floor(column * (1.0 / BLK))
            lon_cell = column - BLK * lat_cell
            lat_place = BLK * a + lat_cell + 0.5 - 0.5 * BLK
            lon_place = BLK * b + lon_cell + 0.5 - 0.5 * BLK
            weight = jnp.exp(-(lat_place * lat_place + lon_place * lon_place) / (2.0 * BLK * BLK))
            weight = jnp.sum(jnp.where(eye, weight, 0.0), axis=1, keepdims=True)
            rows = ref[b + 1, 0:conv, :]
            scaled = (weight * rows.astype(F32)).astype(BF16)
            at = ((a + 1) * 3 + b + 1) * conv
            scaled_ref[at : at + conv, :] = scaled
            spread_ref[at : at + conv, :] = rows
            drive = drive + dot(jnp.broadcast_to(misfit, (8, conv)), scaled)
    drive_ref[...] = drive[0:1]
    gram_ref[...] = transposed_dot(scaled_ref[...], spread_ref[...])


def root_and_apply(gram, drive, mean_ref, anomaly_ref, out_ref):
    members = gram.shape[0]
    eye = lax.broadcasted_iota(jnp.int32, gram.shape, 0) == lax.broadcasted_iota(
        jnp.int32, gram.shape, 1
    )
    system = gram + jnp.where(eye, members - 1.0, 0.0)
    square = jnp.sum(jnp.sum(system * system, axis=0, keepdims=True), axis=1, keepdims=True)
    inverse_scale = lax.rsqrt(square)
    power1 = system * inverse_scale
    half1 = power1.astype(BF16)
    power2 = dot(half1, half1)
    half2 = power2.astype(BF16)
    power3 = dot(half1, half2)
    power4 = dot(half2, half2)
    product = 2.25 * power1 - 1.5 * power2 + 0.25 * power3
    excess = -0.75 * (power1 + product) + 0.25 * (2.25 * power2 - 1.5 * power3 + 0.25 * power4)
    half_excess = excess.astype(BF16)
    lifted = 4.5 * excess + dot(half_excess, half_excess)
    product = 5.0625 * power1 + dot(half1, lifted.astype(BF16))
    inverse_root = 1.5 * excess - 1.125 * product - 0.5 * dot(product.astype(BF16), half_excess)
    inverse_root = inverse_root + jnp.where(eye, 3.375, 0.0)
    first = jnp.sum(inverse_root * drive, axis=1, keepdims=True)
    weight = jnp.sum(inverse_root * first, axis=0, keepdims=True) * inverse_scale
    transform = (jnp.sqrt((members - 1.0) * inverse_scale) * inverse_root + weight).astype(BF16)
    out_ref[...] = mean_ref[...] + dot(transform, anomaly_ref[...])


def final_body(slots_ref, conv_ref, drive_ref, mean_ref, anomaly_ref, out_ref, rows_ref):
    blocks, pieces = slots_ref.shape[0], out_ref.shape[0] // LANES
    count = (slots_ref.shape[1] - PAD) // pieces
    for part in range(pieces):
        rows_ref[:, part * LANES : (part + 1) * LANES] = slots_ref[
            :, part * count : (part + 1) * count, :
        ].reshape(blocks * count, LANES)
    rows = rows_ref[...]
    gram = conv_ref[...] + transposed_dot(rows, rows)
    extra = jnp.sum(slots_ref[:, pieces * count :, :].astype(F32), axis=0)
    extra = extra[0:pieces] + extra[pieces : 2 * pieces]
    extra = jnp.concatenate([extra[part : part + 1] for part in range(pieces)], axis=1)
    root_and_apply(gram, drive_ref[...] + extra, mean_ref, anomaly_ref, out_ref)


def shards(
    background, conv_pert, conv_misfit, conv_column, sat_pert, sat_misfit, sat_rows, sat_targets
):
    members, cells = background.shape[2:]
    conv = conv_pert.shape[2]
    tiles, obs = sat_pert.shape[1:3]
    blocks, bands = lax.axis_size("lon"), lax.axis_size("lat")
    shape = jax.ShapeDtypeStruct

    extra = jnp.concatenate([conv_misfit[0], conv_column[0].astype(BF16)], axis=1)
    extra = jnp.pad(extra, ((0, PAD - 1), (0, members - 2 * conv)))
    own = jnp.concatenate([conv_pert[0, 0], extra], axis=0)
    east = [(i, (i + 1) % blocks) for i in range(blocks)]
    west = [(target, source) for source, target in east]
    low = lax.ppermute(own, "lon", east)
    high = lax.ppermute(own, "lon", west)

    slots = call(
        route_body,
        shape((blocks, members // LANES * 2 * obs + PAD, LANES), BF16),
        [VMEM, VMEM, SMEM, SMEM],
        [pltpu.SMEM((2 * blocks,), jnp.int32), pltpu.SMEM((blocks,), jnp.int32)],
    )(sat_pert[0], sat_misfit[0], sat_rows[0], sat_targets.reshape(-1))

    low, high, slots = lax.optimization_barrier((low, high, slots))
    middle = jnp.stack([low, own, high])
    up = [(i, i + 1) for i in range(bands - 1)]
    down = [(target, source) for source, target in up]
    south = lax.ppermute(middle, "lat", up)
    north = lax.ppermute(middle, "lat", down)
    slots = lax.all_to_all(slots, "lon", 0, 0, tiled=True)

    anomaly, mean = call(
        background_body, (shape((members, cells), BF16), shape((1, cells), F32)), [VMEM]
    )(background[0, 0])
    gram_conv, drive_conv = call(
        conv_body,
        (shape((members, members), F32), shape((1, members), F32)),
        [VMEM] * 3,
        [pltpu.VMEM((9 * conv, members), BF16), pltpu.VMEM((9 * conv, members), BF16)],
    )(middle, south, north)
    result = call(
        final_body,
        shape((members, cells), F32),
        [VMEM] * 5,
        [pltpu.VMEM((blocks * 2 * obs, members), BF16)],
    )(slots, gram_conv, drive_conv, mean, anomaly)
    return result[None, None]


def solution(mesh):
    placed = (
        P("lat", "lon", None, None),
        P("lat", "lon", None, None),
        P("lat", "lon", None),
        P("lat", "lon", None),
        P("lat", "lon", None, None),
        P("lat", "lon", None),
        P("lat", "lon"),
        P("lat", "lon", None),
    )
    return jax.shard_map(
        shards, mesh=mesh, in_specs=placed, out_specs=P("lat", "lon", None, None), check_vma=False
    )
```

```python
import functools

import jax
import jax.numpy as jnp
from jax import lax
from jax.experimental import pallas as pl
from jax.experimental.pallas import tpu as pltpu
from jax.sharding import PartitionSpec as P

BLK = 16
LOC = 2
F32 = jnp.float32
BF16 = jnp.bfloat16
PAD = 16
LANES = 128
MATES = 3
OFFSETS = (4, 3, -3, 2, -2, 1, -1, 0)
CHUNKS = ((0, 1), (1, 3), (3, 8))
VMEM = pltpu.VMEM
SMEM = pltpu.SMEM
LIMIT = 48 * 1024 * 1024


def call(body, outs, in_spaces, scratch=(), flops=0, moved=0):
    return pl.pallas_call(
        body,
        out_shape=outs,
        in_specs=[pl.BlockSpec(memory_space=space) for space in in_spaces],
        out_specs=jax.tree.map(lambda _: pl.BlockSpec(memory_space=VMEM), outs),
        scratch_shapes=list(scratch),
        compiler_params=pltpu.CompilerParams(vmem_limit_bytes=LIMIT),
        cost_estimate=pl.CostEstimate(flops=flops, bytes_accessed=moved, transcendentals=0),
    )


def transposed_dot(left, right):
    return lax.dot_general(left, right, (((0,), (0,)), ((), ())), preferred_element_type=F32)


def dot(left, right):
    return jnp.dot(left, right, preferred_element_type=F32)


def background_body(ensemble_ref, anomaly_ref, mean_ref):
    values = ensemble_ref[...].astype(F32)
    mean = jnp.mean(values, axis=0, keepdims=True)
    mean_ref[...] = mean
    anomaly_ref[...] = (values - mean).astype(BF16)


def route_body(
    pert_hbm, misfit_hbm, rows_hbm, targets_hbm, conv_hbm, conv_misfit_hbm, conv_column_hbm, *refs
):
    outs, halo_ref = refs[: 1 + MATES * len(CHUNKS)], refs[1 + MATES * len(CHUNKS)]
    (
        pert_ref, misfit_ref, rows_ref, targets_ref, conv_misfit_ref, conv_column_ref,
        entry_ref, count_ref, sems,
    ) = refs[2 + MATES * len(CHUNKS) :]
    tiles, obs, members = pert_ref.shape
    conv = conv_hbm.shape[0]
    blocks = count_ref.shape[0]
    planes, columns = blocks // (MATES + 1), MATES + 1
    copies = [
        pltpu.make_async_copy(source, place, sems.at[i])
        for i, (source, place) in enumerate(
            (
                (targets_hbm, targets_ref),
                (rows_hbm, rows_ref),
                (pert_hbm, pert_ref),
                (misfit_hbm, misfit_ref),
                (conv_misfit_hbm, conv_misfit_ref),
                (conv_column_hbm, conv_column_ref),
                (conv_hbm, halo_ref.at[0:conv]),
            )
        )
    ]
    for copy in copies:
        copy.start()

    def clear(block, _):
        count_ref[block] = 0
        entry_ref[2 * block] = -1
        entry_ref[2 * block + 1] = -1
        return 0

    lax.fori_loop(0, blocks, clear, 0, unroll=True)
    copies[0].wait()
    copies[1].wait()
    for tile in range(tiles):
        for k in range(LOC):
            block = targets_ref[k, tile]
            used = count_ref[block]
            entry_ref[2 * block + used] = LOC * tile + k
            count_ref[block] = used + 1
    for copy in copies[2:]:
        copy.wait()
    row = lax.broadcasted_iota(jnp.int32, (obs, members), 0)
    me = lax.axis_index("lon")
    plane, column = me // columns, me % columns
    places = []
    for mate in range(columns):
        for at, offset in enumerate(OFFSETS):
            if mate == 0:
                ref, index = outs[0], at
            else:
                chunk = [at in range(low, high) for low, high in CHUNKS].index(True)
                ref, index = outs[1 + (mate - 1) * len(CHUNKS) + chunk], at - CHUNKS[chunk][0]
            there = (plane + offset + planes) % planes
            places.append((ref, index, there * columns + (column ^ mate)))
    for ref, index, block in places:
        for slot in range(2):
            entry = entry_ref[2 * block + slot]
            safe = jnp.maximum(entry, 0)
            tile = safe // LOC
            live = jnp.where(entry >= 0, rows_ref[0, tile], 0)
            factor = jnp.where(safe % LOC == 0, 1.0, 0.5**0.5).astype(F32)
            values = pert_ref[tile].astype(F32) * factor
            values = jnp.where(row < live, values, 0.0).astype(BF16)
            for part in range(members // LANES):
                start = part * 2 * obs + slot * obs
                ref[index, start : start + obs, :] = values[:, part * LANES : (part + 1) * LANES]

    total = tiles * obs
    lane = lax.broadcasted_iota(jnp.int32, (1, total), 1)
    own_tile = lane // obs
    live = jnp.zeros((1, total), jnp.int32)
    named = [jnp.zeros((1, total), jnp.int32) for _ in range(LOC)]
    for tile in range(tiles):
        here = own_tile == tile
        live = jnp.where(here, rows_ref[0, tile], live)
        for k in range(LOC):
            named[k] = jnp.where(here, targets_ref[k, tile], named[k])
    repeat = (
        lax.broadcasted_iota(jnp.int32, (obs, total), 1) % obs
        == lax.broadcasted_iota(jnp.int32, (obs, total), 0)
    )
    spread = dot(misfit_ref[...], jnp.where(repeat, 1.0, 0.0).astype(BF16))
    pick = lax.broadcasted_iota(jnp.int32, (tiles, total), 1) // obs == lax.broadcasted_iota(
        jnp.int32, (tiles, total), 0
    )
    misfit = jnp.sum(jnp.where(pick, spread, 0.0), axis=0, keepdims=True)
    misfit = jnp.where(lane % obs < live, misfit, 0.0)
    position = lax.broadcasted_iota(jnp.int32, (blocks, 1), 0)
    block = jnp.zeros((blocks, 1), jnp.int32)
    for at, (_, _, there) in enumerate(places):
        block = jnp.where(position == at, there, block)
    weight = jnp.zeros((blocks, total), F32)
    for k in range(LOC):
        weight = weight + jnp.where(block == named[k], 0.5**k, 0.0)
    drive = dot((weight * misfit).astype(BF16), pert_ref[...].reshape(total, members))
    upper = drive.astype(BF16).astype(F32)
    empty = jnp.zeros((PAD - 2 * (members // LANES), LANES), F32)
    for at, (ref, index, _) in enumerate(places):
        parts = [
            piece[at : at + 1, part * LANES : (part + 1) * LANES]
            for piece in (upper, drive - upper)
            for part in range(members // LANES)
        ]
        ref[index, members // LANES * 2 * obs :, :] = jnp.concatenate(parts + [empty]).astype(BF16)
    first = lax.broadcasted_iota(jnp.int32, (PAD, conv), 0) == 0
    halo_ref[conv:, :] = jnp.zeros((PAD, members), BF16)
    halo_ref[conv:, 0:conv] = jnp.where(first, conv_misfit_ref[...].astype(F32), 0.0).astype(BF16)
    halo_ref[conv:, conv : 2 * conv] = jnp.where(
        first, conv_column_ref[...].astype(F32), 0.0
    ).astype(BF16)


def gather_rows(own_ref, at, mates, index, rows_ref):
    sources = [(own_ref, at)] + [(ref, index) for ref in mates]
    pieces = rows_ref.shape[1] // LANES
    count = (own_ref.shape[1] - PAD) // pieces
    drive = jnp.zeros((PAD, LANES), F32)
    for number, (ref, place) in enumerate(sources):
        for part in range(pieces):
            rows_ref[number * count : (number + 1) * count, part * LANES : (part + 1) * LANES] = ref[
                place, part * count : (part + 1) * count, :
            ]
        drive = drive + ref[place, pieces * count :, :].astype(F32)
    return drive


def triangle(size=LANES):
    across = lax.broadcasted_iota(jnp.int32, (size, size), 1)
    down = lax.broadcasted_iota(jnp.int32, (size, size), 0)
    return down, across


def packed(rows_ref, drive):
    down, across = triangle()
    pieces = rows_ref.shape[1] // LANES
    bands = []
    for part in range(pieces):
        left = rows_ref[:, part * LANES : (part + 1) * LANES]
        bands.append(transposed_dot(left, rows_ref[:, part * LANES :]))
    blocks, diagonals = [], []
    for part in range(0, pieces, 2):
        lower = bands[part + 1][:, 0:LANES]
        blocks.append(jnp.where(down <= across, bands[part][:, 0:LANES], lower))
        diagonals.append(jnp.sum(jnp.where(down == across, lower, 0.0), axis=0, keepdims=True))
    for part in range(pieces):
        for other in range(1, pieces - part):
            blocks.append(bands[part][:, other * LANES : (other + 1) * LANES])
    total = drive[0:pieces] + drive[pieces : 2 * pieces]
    empty = jnp.zeros((PAD - 2 * pieces - len(diagonals), LANES), F32)
    return blocks, total, jnp.concatenate(diagonals), empty


def split_drive(total, diagonals, empty):
    upper = total.astype(BF16).astype(F32)
    return jnp.concatenate([upper, total - upper, diagonals, empty]).astype(BF16)


def extra_of(extra, pieces):
    extra = extra.astype(F32)
    return extra[0:pieces] + extra[pieces : 2 * pieces], extra[2 * pieces : 2 * pieces + pieces // 2]


def open_body(own_ref, mate1_ref, mate2_ref, mate3_ref, up_ref, down_ref, rows_ref):
    drive = gather_rows(own_ref, 0, (mate1_ref, mate2_ref, mate3_ref), 0, rows_ref)
    blocks, total, diagonals, empty = packed(rows_ref, drive)
    half = len(blocks) // 2
    for number, block in enumerate(blocks):
        ref, place = (up_ref, number) if number < half else (down_ref, number - half)
        ref[place * LANES : (place + 1) * LANES, :] = block.astype(BF16)
    down_ref[half * LANES :, :] = split_drive(total, diagonals, empty)


def step_body(at, index, own_ref, mate1_ref, mate2_ref, mate3_ref, up_in, down_in, up_ref, down_ref, rows_ref):
    mates = (mate1_ref, mate2_ref, mate3_ref)
    pieces = rows_ref.shape[1] // LANES
    for which, (came, out) in enumerate(((up_in, up_ref), (down_in, down_ref))):
        drive = gather_rows(own_ref, at + which, mates, index + which, rows_ref)
        blocks, total, diagonals, empty = packed(rows_ref, drive)
        skip = 0
        whole = came.shape == out.shape
        if not whole and which == 1:
            skip = len(blocks) - came.shape[0] // LANES
        for number, block in enumerate(blocks):
            place = (number - skip) * LANES
            if 0 <= place and place + LANES <= came.shape[0]:
                block = block + came[place : place + LANES, :].astype(F32)
            out[number * LANES : (number + 1) * LANES, :] = block.astype(BF16)
        if whole or which == 1:
            more, more_diagonals = extra_of(came[came.shape[0] - PAD :, :], pieces)
            total, diagonals = total + more, diagonals + more_diagonals
        out[len(blocks) * LANES :, :] = split_drive(total, diagonals, empty)


def conv_body(middle_ref, south_ref, north_ref, gram_ref, drive_ref, scaled_ref, spread_ref):
    conv, members = middle_ref.shape[1] - PAD, middle_ref.shape[2]
    eye = lax.broadcasted_iota(jnp.int32, (conv, conv), 0) == lax.broadcasted_iota(
        jnp.int32, (conv, conv), 1
    )
    drive = jnp.zeros((8, members), F32)
    for a, ref in ((-1, south_ref), (0, middle_ref), (1, north_ref)):
        for b in (-1, 0, 1):
            misfit = ref[b + 1, conv : conv + 1, 0:conv]
            column = ref[b + 1, conv : conv + 1, conv : 2 * conv].astype(F32)
            lat_cell = jnp.floor(column * (1.0 / BLK))
            lon_cell = column - BLK * lat_cell
            lat_place = BLK * a + lat_cell + 0.5 - 0.5 * BLK
            lon_place = BLK * b + lon_cell + 0.5 - 0.5 * BLK
            weight = jnp.exp(-(lat_place * lat_place + lon_place * lon_place) / (2.0 * BLK * BLK))
            weight = jnp.sum(jnp.where(eye, weight, 0.0), axis=1, keepdims=True)
            rows = ref[b + 1, 0:conv, :]
            scaled = (weight * rows.astype(F32)).astype(BF16)
            at = ((a + 1) * 3 + b + 1) * conv
            scaled_ref[at : at + conv, :] = scaled
            spread_ref[at : at + conv, :] = rows
            drive = drive + dot(jnp.broadcast_to(misfit, (8, conv)), scaled)
    drive_ref[...] = drive[0:1]
    gram_ref[...] = transposed_dot(scaled_ref[...], spread_ref[...])


def root_and_apply(gram, drive, mean_ref, anomaly_ref, out_ref):
    members = gram.shape[0]
    eye = lax.broadcasted_iota(jnp.int32, gram.shape, 0) == lax.broadcasted_iota(
        jnp.int32, gram.shape, 1
    )
    system = gram + jnp.where(eye, members - 1.0, 0.0)
    square = jnp.sum(jnp.sum(system * system, axis=0, keepdims=True), axis=1, keepdims=True)
    inverse_scale = lax.rsqrt(square)
    power1 = system * inverse_scale
    half1 = power1.astype(BF16)
    power2 = dot(half1, half1)
    half2 = power2.astype(BF16)
    power3 = dot(half1, half2)
    power4 = dot(half2, half2)
    product = 2.25 * power1 - 1.5 * power2 + 0.25 * power3
    excess = -0.75 * (power1 + product) + 0.25 * (2.25 * power2 - 1.5 * power3 + 0.25 * power4)
    half_excess = excess.astype(BF16)
    lifted = 4.5 * excess + dot(half_excess, half_excess)
    product = 5.0625 * power1 + dot(half1, lifted.astype(BF16))
    inverse_root = 1.5 * excess - 1.125 * product - 0.5 * dot(product.astype(BF16), half_excess)
    inverse_root = inverse_root + jnp.where(eye, 3.375, 0.0)
    first = jnp.sum(inverse_root * drive, axis=1, keepdims=True)
    weight = jnp.sum(inverse_root * first, axis=0, keepdims=True) * inverse_scale
    transform = (jnp.sqrt((members - 1.0) * inverse_scale) * inverse_root + weight).astype(BF16)
    out_ref[...] = mean_ref[...] + dot(transform, anomaly_ref[...])


def final_body(
    at, index, own_ref, mate1_ref, mate2_ref, mate3_ref, up_ref, down_ref,
    conv_ref, drive_ref, mean_ref, anomaly_ref, out_ref, rows_ref, gram_ref,
):
    pieces = rows_ref.shape[1] // LANES
    drive = gather_rows(own_ref, at, (mate1_ref, mate2_ref, mate3_ref), index, rows_ref)
    rows = rows_ref[...]
    gram_ref[...] = conv_ref[...] + transposed_dot(rows, rows)
    total = drive[0:pieces] + drive[pieces : 2 * pieces]
    diagonals = jnp.zeros((pieces // 2, LANES), F32)
    for ref in (up_ref, down_ref):
        more, more_diagonals = extra_of(ref[ref.shape[0] - PAD :, :], pieces)
        total, diagonals = total + more, diagonals + more_diagonals
    down, across = triangle()

    def add(part, other, block):
        place = (slice(part * LANES, (part + 1) * LANES), slice(other * LANES, (other + 1) * LANES))
        gram_ref[place] = gram_ref[place] + block

    number = 0

    def block_of(number):
        place = slice(number * LANES, (number + 1) * LANES)
        return up_ref[place, :].astype(F32) + down_ref[place, :].astype(F32)

    for part in range(0, pieces, 2):
        block = block_of(number)
        turned = block.T
        add(part, part, jnp.where(down <= across, block, turned))
        middle = jnp.where(down == across, diagonals[number : number + 1], turned)
        add(part + 1, part + 1, jnp.where(down > across, block, middle))
        number += 1
    for part in range(pieces):
        for other in range(part + 1, pieces):
            block = block_of(number)
            add(part, other, block)
            add(other, part, block.T)
            number += 1
    total = jnp.concatenate([total[part : part + 1] for part in range(pieces)], axis=1)
    root_and_apply(gram_ref[...], drive_ref[...] + total, mean_ref, anomaly_ref, out_ref)


def shards(
    background, conv_pert, conv_misfit, conv_column, sat_pert, sat_misfit, sat_rows, sat_targets
):
    members, cells = background.shape[2:]
    conv = conv_pert.shape[2]
    tiles, obs = sat_pert.shape[1:3]
    blocks, bands = lax.axis_size("lon"), lax.axis_size("lat")
    shape = jax.ShapeDtypeStruct

    pieces = members // LANES
    packet = pieces * 2 * obs + PAD
    triangles = pieces * pieces // 2
    full = triangles * LANES + PAD
    half = triangles // 2 * LANES
    columns = MATES + 1

    def ring(values, step):
        return lax.ppermute(values, "lon", [(i, (i + step * columns) % blocks) for i in range(blocks)])

    def trade(values, mate):
        return lax.ppermute(values, "lon", [(i, i ^ mate) for i in range(blocks)])

    outs = [shape((len(OFFSETS), packet, LANES), BF16)]
    for mate in range(MATES):
        outs += [shape((high - low, packet, LANES), BF16) for low, high in CHUNKS]
    outs.append(shape((conv + PAD, members), BF16))
    own, *sends, halo = call(
        route_body,
        tuple(outs),
        [pl.ANY] * 7,
        [
            pltpu.VMEM((tiles, obs, members), BF16),
            pltpu.VMEM((tiles, obs), BF16),
            pltpu.SMEM((1, tiles), jnp.int32),
            pltpu.SMEM((LOC, tiles), jnp.int32),
            pltpu.VMEM((1, conv), BF16),
            pltpu.VMEM((1, conv), jnp.int32),
            pltpu.SMEM((2 * blocks,), jnp.int32),
            pltpu.SMEM((blocks,), jnp.int32),
            pltpu.SemaphoreType.DMA((7,)),
        ],
    )(
        sat_pert[0], sat_misfit[0], sat_rows, jnp.swapaxes(sat_targets[0], 0, 1),
        conv_pert[0, 0], conv_misfit[0], conv_column[0],
    )
    chunked = [[sends[mate * len(CHUNKS) + c] for mate in range(MATES)] for c in range(len(CHUNKS))]
    got = []
    for c, chunk in enumerate(chunked):
        if c:
            tied = lax.optimization_barrier(tuple(got[-1]) + tuple(chunk))
            got[-1], chunk = tied[:MATES], tied[MATES:]
        got.append([trade(values, mate + 1) for mate, values in enumerate(chunk)])

    east = [(i, (i + 1) % blocks) for i in range(blocks)]
    west = [(target, source) for source, target in east]
    low = lax.ppermute(halo, "lon", east)
    high = lax.ppermute(halo, "lon", west)
    middle = jnp.stack([low, halo, high])
    north = [(i, i + 1) for i in range(bands - 1)]
    south = [(target, source) for source, target in north]
    below = lax.ppermute(middle, "lat", north)
    above = lax.ppermute(middle, "lat", south)

    scratch = [pltpu.VMEM((2 * obs * columns, members), BF16)]
    up, down = call(
        open_body, (shape((half, LANES), BF16), shape((full - half, LANES), BF16)), [VMEM] * 4, scratch
    )(own, *got[0])
    for step, (at, c) in enumerate(((1, 1), (3, 2), (5, 2))):
        up, down = ring(up, 1), ring(down, -1)
        up, down = call(
            functools.partial(step_body, at, at - CHUNKS[c][0]),
            (shape((full, LANES), BF16), shape((full, LANES), BF16)),
            [VMEM] * 6,
            scratch,
        )(own, *got[c], up, down)
    up, down = ring(up, 1), ring(down, -1)

    anomaly, mean = call(
        background_body, (shape((members, cells), BF16), shape((1, cells), F32)), [VMEM]
    )(background[0, 0])
    gram_conv, drive_conv = call(
        conv_body,
        (shape((members, members), F32), shape((1, members), F32)),
        [VMEM] * 3,
        [pltpu.VMEM((9 * conv, members), BF16), pltpu.VMEM((9 * conv, members), BF16)],
    )(middle, below, above)
    result = call(
        functools.partial(final_body, 7, 7 - CHUNKS[2][0]),
        shape((members, cells), F32),
        [VMEM] * 10,
        scratch + [pltpu.VMEM((members, members), F32)],
    )(own, *got[2], up, down, gram_conv, drive_conv, mean, anomaly)
    return result[None, None]


def solution(mesh):
    placed = (
        P("lat", "lon", None, None),
        P("lat", "lon", None, None),
        P("lat", "lon", None),
        P("lat", "lon", None),
        P("lat", "lon", None, None),
        P("lat", "lon", None),
        P("lat", "lon"),
        P("lat", "lon", None),
    )
    return jax.shard_map(
        shards, mesh=mesh, in_specs=placed, out_specs=P("lat", "lon", None, None), check_vma=False
    )
```

```python
import functools

import jax
import jax.numpy as jnp
from jax import lax
from jax.experimental import pallas as pl
from jax.experimental.pallas import tpu as pltpu
from jax.sharding import PartitionSpec as P

BLK = 16
LOC = 2
F32 = jnp.float32
BF16 = jnp.bfloat16
PAD = 16
LANES = 128
COLUMNS = 4
OFFSETS = (4, 3, -3, 2, -2, 1, -1, 0)
CHUNKS = ((0, 1), (1, 8))
VMEM = pltpu.VMEM
SMEM = pltpu.SMEM
LIMIT = 48 * 1024 * 1024


def call(body, outs, in_spaces, scratch=(), limit=LIMIT, flops=0, moved=0):
    return pl.pallas_call(
        body,
        out_shape=outs,
        in_specs=[pl.BlockSpec(memory_space=space) for space in in_spaces],
        out_specs=jax.tree.map(lambda _: pl.BlockSpec(memory_space=VMEM), outs),
        scratch_shapes=list(scratch),
        compiler_params=pltpu.CompilerParams(vmem_limit_bytes=limit),
        cost_estimate=pl.CostEstimate(flops=flops, bytes_accessed=moved, transcendentals=0),
    )


def transposed_dot(left, right):
    return lax.dot_general(left, right, (((0,), (0,)), ((), ())), preferred_element_type=F32)


def dot(left, right):
    return jnp.dot(left, right, preferred_element_type=F32)


def background_body(ensemble_ref, anomaly_ref, mean_ref):
    values = ensemble_ref[...].astype(F32)
    mean = jnp.mean(values, axis=0, keepdims=True)
    mean_ref[...] = mean
    anomaly_ref[...] = (values - mean).astype(BF16)


def halo_body(conv_hbm, misfit_hbm, column_hbm, halo_ref, misfit_ref, column_ref, sems):
    conv, members = conv_hbm.shape
    copies = [
        pltpu.make_async_copy(misfit_hbm, misfit_ref, sems.at[0]),
        pltpu.make_async_copy(column_hbm, column_ref, sems.at[1]),
        pltpu.make_async_copy(conv_hbm, halo_ref.at[0:conv], sems.at[2]),
    ]
    for copy in copies:
        copy.start()
    first = lax.broadcasted_iota(jnp.int32, (PAD, conv), 0) == 0
    halo_ref[conv:, :] = jnp.zeros((PAD, members), BF16)
    copies[0].wait()
    copies[1].wait()
    halo_ref[conv:, 0:conv] = jnp.where(first, misfit_ref[...].astype(F32), 0.0).astype(BF16)
    halo_ref[conv:, conv : 2 * conv] = jnp.where(first, column_ref[...].astype(F32), 0.0).astype(BF16)
    copies[2].wait()


def route_body(
    pert0_hbm, pert1_hbm, misfit0_hbm, misfit1_hbm, lists0_hbm, lists1_hbm, own_ref, *refs
):
    sends = refs[: len(CHUNKS)]
    pert_ref, misfit_ref, lists_ref, entry_ref, count_ref, sems = refs[len(CHUNKS) :]
    tiles, obs, members = pert0_hbm.shape
    blocks = count_ref.shape[0]
    copies = []
    for source, (pert, misfit, lists) in enumerate(
        ((pert0_hbm, misfit0_hbm, lists0_hbm), (pert1_hbm, misfit1_hbm, lists1_hbm))
    ):
        span = pl.ds(source * tiles, tiles)
        copies.append(pltpu.make_async_copy(lists, lists_ref.at[source], sems.at[3 * source]))
        copies.append(pltpu.make_async_copy(misfit, misfit_ref.at[span], sems.at[3 * source + 1]))
        copies.append(pltpu.make_async_copy(pert, pert_ref.at[span], sems.at[3 * source + 2]))
    for copy in copies:
        copy.start()

    def clear(block, _):
        count_ref[block] = 0
        for slot in range(4):
            entry_ref[4 * block + slot] = -1
        return 0

    lax.fori_loop(0, blocks, clear, 0, unroll=True)
    copies[0].wait()
    copies[3].wait()
    for source in range(2):
        for tile in range(tiles):
            for k in range(LOC):
                block = lists_ref[source, k, tile]
                used = count_ref[block]
                entry_ref[4 * block + used] = LOC * (tiles * source + tile) + k
                count_ref[block] = used + 1
    for at in (1, 2, 4, 5):
        copies[at].wait()
    row = lax.broadcasted_iota(jnp.int32, (obs, members), 0)
    me = lax.axis_index("lon")
    planes = blocks // COLUMNS
    plane, column = me // COLUMNS, me % COLUMNS
    places = []
    for mate in range(2):
        for at, offset in enumerate(OFFSETS):
            ref, index = own_ref, at
            if mate:
                chunk = [at in range(low, high) for low, high in CHUNKS].index(True)
                ref, index = sends[chunk], at - CHUNKS[chunk][0]
            there = (plane + offset + planes) % planes
            places.append((ref, index, there * COLUMNS + (column ^ mate)))
    pieces = members // LANES
    for ref, index, block in places:
        for slot in range(4):
            entry = entry_ref[4 * block + slot]
            safe = jnp.maximum(entry, 0)
            tile = safe // LOC
            source = jnp.where(tile >= tiles, 1, 0)
            live = jnp.where(entry >= 0, lists_ref[source, LOC, tile - tiles * source], 0)
            factor = jnp.where(safe % LOC == 0, 1.0, 0.5**0.5).astype(F32)
            values = pert_ref[tile].astype(F32) * factor
            values = jnp.where(row < live, values, 0.0).astype(BF16)
            for part in range(pieces):
                start = (part * 4 + slot) * obs
                ref[index, start : start + obs, :] = values[:, part * LANES : (part + 1) * LANES]

    total = 2 * tiles * obs
    lane = lax.broadcasted_iota(jnp.int32, (1, total), 1)
    own_tile = lane // obs
    live = jnp.zeros((1, total), jnp.int32)
    named = [jnp.zeros((1, total), jnp.int32) for _ in range(LOC)]
    for source in range(2):
        for tile in range(tiles):
            here = own_tile == source * tiles + tile
            live = jnp.where(here, lists_ref[source, LOC, tile], live)
            for k in range(LOC):
                named[k] = jnp.where(here, lists_ref[source, k, tile], named[k])
    repeat = (
        lax.broadcasted_iota(jnp.int32, (obs, total), 1) % obs
        == lax.broadcasted_iota(jnp.int32, (obs, total), 0)
    )
    spread = dot(misfit_ref[...], jnp.where(repeat, 1.0, 0.0).astype(BF16))
    pick = lax.broadcasted_iota(jnp.int32, (2 * tiles, total), 1) // obs == lax.broadcasted_iota(
        jnp.int32, (2 * tiles, total), 0
    )
    misfit = jnp.sum(jnp.where(pick, spread, 0.0), axis=0, keepdims=True)
    misfit = jnp.where(lane % obs < live, misfit, 0.0)
    position = lax.broadcasted_iota(jnp.int32, (len(places), 1), 0)
    block = jnp.zeros((len(places), 1), jnp.int32)
    for at, (_, _, there) in enumerate(places):
        block = jnp.where(position == at, there, block)
    weight = jnp.zeros((len(places), total), F32)
    for k in range(LOC):
        weight = weight + jnp.where(block == named[k], 0.5**k, 0.0)
    drive = dot((weight * misfit).astype(BF16), pert_ref[...].reshape(total, members))
    upper = drive.astype(BF16).astype(F32)
    empty = jnp.zeros((PAD - 2 * pieces, LANES), F32)
    for at, (ref, index, _) in enumerate(places):
        parts = [
            piece[at : at + 1, part * LANES : (part + 1) * LANES]
            for piece in (upper, drive - upper)
            for part in range(pieces)
        ]
        ref[index, 4 * obs * pieces :, :] = jnp.concatenate(parts + [empty]).astype(BF16)


def gather_rows(own_ref, at, mate_ref, index, rows_ref):
    sources = [(own_ref, at), (mate_ref, index)]
    pieces = rows_ref.shape[1] // LANES
    count = (own_ref.shape[1] - PAD) // pieces
    drive = jnp.zeros((PAD, LANES), F32)
    for number, (ref, place) in enumerate(sources):
        for part in range(pieces):
            rows_ref[number * count : (number + 1) * count, part * LANES : (part + 1) * LANES] = ref[
                place, part * count : (part + 1) * count, :
            ]
        drive = drive + ref[place, pieces * count :, :].astype(F32)
    return drive


def triangle(size=LANES):
    across = lax.broadcasted_iota(jnp.int32, (size, size), 1)
    down = lax.broadcasted_iota(jnp.int32, (size, size), 0)
    return down, across


def packed(rows_ref, drive, right_ref=None):
    down, across = triangle()
    right_ref = rows_ref if right_ref is None else right_ref
    pieces = rows_ref.shape[1] // LANES
    bands = []
    for part in range(pieces):
        left = rows_ref[:, part * LANES : (part + 1) * LANES]
        bands.append(transposed_dot(left, right_ref[:, part * LANES :]))
    blocks, diagonals = [], []
    for part in range(0, pieces, 2):
        lower = bands[part + 1][:, 0:LANES]
        blocks.append(jnp.where(down <= across, bands[part][:, 0:LANES], lower))
        diagonals.append(jnp.sum(jnp.where(down == across, lower, 0.0), axis=0, keepdims=True))
    for part in range(pieces):
        for other in range(1, pieces - part):
            blocks.append(bands[part][:, other * LANES : (other + 1) * LANES])
    total = drive[0:pieces] + drive[pieces : 2 * pieces]
    empty = jnp.zeros((PAD - 2 * pieces - len(diagonals), LANES), F32)
    return blocks, total, jnp.concatenate(diagonals), empty


def split_drive(total, diagonals, empty):
    upper = total.astype(BF16).astype(F32)
    return jnp.concatenate([upper, total - upper, diagonals, empty]).astype(BF16)


def extra_of(extra, pieces):
    extra = extra.astype(F32)
    return extra[0:pieces] + extra[pieces : 2 * pieces], extra[2 * pieces : 2 * pieces + pieces // 2]


def open_body(own_ref, mate_ref, up_ref, down_ref, rows_ref):
    drive = gather_rows(own_ref, 0, mate_ref, 0, rows_ref)
    blocks, total, diagonals, empty = packed(rows_ref, drive)
    half = len(blocks) // 2
    for number, block in enumerate(blocks):
        ref, place = (up_ref, number) if number < half else (down_ref, number - half)
        ref[place * LANES : (place + 1) * LANES, :] = block.astype(BF16)
    down_ref[half * LANES :, :] = split_drive(total, diagonals, empty)


def step_body(at, index, own_ref, mate_ref, up_in, down_in, up_ref, down_ref, rows_ref):
    pieces = rows_ref.shape[1] // LANES
    for which, (came, out) in enumerate(((up_in, up_ref), (down_in, down_ref))):
        drive = gather_rows(own_ref, at + which, mate_ref, index + which, rows_ref)
        blocks, total, diagonals, empty = packed(rows_ref, drive)
        skip = 0
        whole = came.shape == out.shape
        if not whole and which == 1:
            skip = len(blocks) - came.shape[0] // LANES
        for number, block in enumerate(blocks):
            place = (number - skip) * LANES
            if 0 <= place and place + LANES <= came.shape[0]:
                block = block + came[place : place + LANES, :].astype(F32)
            out[number * LANES : (number + 1) * LANES, :] = block.astype(BF16)
        if whole or which == 1:
            more, more_diagonals = extra_of(came[came.shape[0] - PAD :, :], pieces)
            total, diagonals = total + more, diagonals + more_diagonals
        out[len(blocks) * LANES :, :] = split_drive(total, diagonals, empty)


def conv_body(
    low_ref, halo_ref, high_ref, gram_ref, drive_ref, north_ref, south_ref, scaled_ref, spread_ref
):
    conv, members = halo_ref.shape[0] - PAD, halo_ref.shape[1]
    pieces = members // LANES
    eye = lax.broadcasted_iota(jnp.int32, (conv, conv), 0) == lax.broadcasted_iota(
        jnp.int32, (conv, conv), 1
    )
    refs = ((-1, low_ref), (0, halo_ref), (1, high_ref))
    for b, ref in refs:
        spread_ref[(b + 1) * conv : (b + 2) * conv, :] = ref[0:conv, :]
    for a, out_ref in ((-1, north_ref), (1, south_ref), (0, gram_ref)):
        drive = jnp.zeros((8, members), F32)
        for b, ref in refs:
            misfit = ref[conv : conv + 1, 0:conv]
            column = ref[conv : conv + 1, conv : 2 * conv].astype(F32)
            lat_cell = jnp.floor(column * (1.0 / BLK))
            lon_cell = column - BLK * lat_cell
            lat_place = BLK * a + lat_cell + 0.5 - 0.5 * BLK
            lon_place = BLK * b + lon_cell + 0.5 - 0.5 * BLK
            weight = jnp.exp(-(lat_place * lat_place + lon_place * lon_place) / (2.0 * BLK * BLK))
            weight = jnp.sum(jnp.where(eye, weight, 0.0), axis=1, keepdims=True)
            scaled = (weight * ref[0:conv, :].astype(F32)).astype(BF16)
            scaled_ref[(b + 1) * conv : (b + 2) * conv, :] = scaled
            drive = drive + dot(jnp.broadcast_to(misfit, (8, conv)), scaled)
        if a == 0:
            drive_ref[...] = drive[0:1]
            gram_ref[...] = transposed_dot(scaled_ref[...], spread_ref[...])
            continue
        total = jnp.concatenate(
            [drive[0:1, part * LANES : (part + 1) * LANES] for part in range(pieces)]
            + [jnp.zeros((PAD - pieces, LANES), F32)]
        )
        blocks, total, diagonals, empty = packed(scaled_ref, total, spread_ref)
        for number, block in enumerate(blocks):
            out_ref[number * LANES : (number + 1) * LANES, :] = block.astype(BF16)
        out_ref[len(blocks) * LANES :, :] = split_drive(total, diagonals, empty)


def root_and_apply(gram, drive, mean_ref, anomaly_ref, out_ref):
    members = gram.shape[0]
    eye = lax.broadcasted_iota(jnp.int32, gram.shape, 0) == lax.broadcasted_iota(
        jnp.int32, gram.shape, 1
    )
    system = gram + jnp.where(eye, members - 1.0, 0.0)
    square = jnp.sum(jnp.sum(system * system, axis=0, keepdims=True), axis=1, keepdims=True)
    inverse_scale = lax.rsqrt(square)
    power1 = system * inverse_scale
    half1 = power1.astype(BF16)
    power2 = dot(half1, half1)
    half2 = power2.astype(BF16)
    power3 = dot(half1, half2)
    power4 = dot(half2, half2)
    product = 2.25 * power1 - 1.5 * power2 + 0.25 * power3
    excess = -0.75 * (power1 + product) + 0.25 * (2.25 * power2 - 1.5 * power3 + 0.25 * power4)
    half_excess = excess.astype(BF16)
    lifted = 4.5 * excess + dot(half_excess, half_excess)
    product = 5.0625 * power1 + dot(half1, lifted.astype(BF16))
    inverse_root = 1.5 * excess - 1.125 * product - 0.5 * dot(product.astype(BF16), half_excess)
    inverse_root = inverse_root + jnp.where(eye, 3.375, 0.0)
    first = jnp.sum(inverse_root * drive, axis=1, keepdims=True)
    weight = jnp.sum(inverse_root * first, axis=0, keepdims=True) * inverse_scale
    transform = (jnp.sqrt((members - 1.0) * inverse_scale) * inverse_root + weight).astype(BF16)
    out_ref[...] = mean_ref[...] + dot(transform, anomaly_ref[...])


def final_body(
    at, index, own_ref, mate_ref, up_ref, down_ref, below_ref, above_ref,
    conv_ref, drive_ref, mean_ref, anomaly_ref, out_ref, rows_ref, gram_ref,
):
    pieces = rows_ref.shape[1] // LANES
    drive = gather_rows(own_ref, at, mate_ref, index, rows_ref)
    rows = rows_ref[...]
    gram_ref[...] = conv_ref[...] + transposed_dot(rows, rows)
    total = drive[0:pieces] + drive[pieces : 2 * pieces]
    diagonals = jnp.zeros((pieces // 2, LANES), F32)
    arrived = (up_ref, down_ref, below_ref, above_ref)
    for ref in arrived:
        more, more_diagonals = extra_of(ref[ref.shape[0] - PAD :, :], pieces)
        total, diagonals = total + more, diagonals + more_diagonals
    down, across = triangle()

    def add(part, other, block):
        place = (slice(part * LANES, (part + 1) * LANES), slice(other * LANES, (other + 1) * LANES))
        gram_ref[place] = gram_ref[place] + block

    number = 0

    def block_of(number):
        place = slice(number * LANES, (number + 1) * LANES)
        return sum(ref[place, :].astype(F32) for ref in arrived)

    for part in range(0, pieces, 2):
        block = block_of(number)
        turned = block.T
        add(part, part, jnp.where(down <= across, block, turned))
        middle = jnp.where(down == across, diagonals[number : number + 1], turned)
        add(part + 1, part + 1, jnp.where(down > across, block, middle))
        number += 1
    for part in range(pieces):
        for other in range(part + 1, pieces):
            block = block_of(number)
            add(part, other, block)
            add(other, part, block.T)
            number += 1
    total = jnp.concatenate([total[part : part + 1] for part in range(pieces)], axis=1)
    root_and_apply(gram_ref[...], drive_ref[...] + total, mean_ref, anomaly_ref, out_ref)


def shards(
    background, conv_pert, conv_misfit, conv_column, sat_pert, sat_misfit, sat_rows, sat_targets
):
    members, cells = background.shape[2:]
    conv = conv_pert.shape[2]
    tiles, obs = sat_pert.shape[1:3]
    blocks, bands = lax.axis_size("lon"), lax.axis_size("lat")
    shape = jax.ShapeDtypeStruct

    pieces = members // LANES
    packet = pieces * 4 * obs + PAD
    triangles = pieces * pieces // 2
    full = triangles * LANES + PAD
    half = triangles // 2 * LANES
    message = shape((full, LANES), BF16)

    def ring(values, step):
        return lax.ppermute(values, "lon", [(i, (i + step * COLUMNS) % blocks) for i in range(blocks)])

    def trade(values, mate):
        return lax.ppermute(values, "lon", [(i, i ^ mate) for i in range(blocks)])

    lists = jnp.concatenate([jnp.swapaxes(sat_targets[0], 0, 1), sat_rows])
    pert1, misfit1, lists1 = trade(sat_pert[0], 2), trade(sat_misfit[0], 2), trade(lists, 2)
    halo = call(
        halo_body,
        shape((conv + PAD, members), BF16),
        [pltpu.HBM] * 3,
        [pltpu.VMEM((1, conv), BF16), pltpu.VMEM((1, conv), jnp.int32), pltpu.SemaphoreType.DMA((3,))],
        limit=None,
    )(conv_pert[0, 0], conv_misfit[0], conv_column[0])
    east = [(i, (i + 1) % blocks) for i in range(blocks)]
    west = [(target, source) for source, target in east]
    low = lax.ppermute(halo, "lon", east)
    high = lax.ppermute(halo, "lon", west)
    gram_conv, drive_conv, to_north, to_south = call(
        conv_body,
        (shape((members, members), F32), shape((1, members), F32), message, message),
        [VMEM] * 3,
        [pltpu.VMEM((3 * conv, members), BF16), pltpu.VMEM((3 * conv, members), BF16)],
    )(low, halo, high)
    to_north, to_south, pert1 = lax.optimization_barrier((to_north, to_south, pert1))
    north = [(i, i + 1) for i in range(bands - 1)]
    south = [(target, source) for source, target in north]
    below = lax.ppermute(to_north, "lat", north)
    above = lax.ppermute(to_south, "lat", south)
    own, *sends = call(
        route_body,
        tuple(
            shape((count, packet, LANES), BF16)
            for count in [len(OFFSETS)] + [high - low for low, high in CHUNKS]
        ),
        [pltpu.HBM] * 6,
        [
            pltpu.VMEM((2 * tiles, obs, members), BF16),
            pltpu.VMEM((2 * tiles, obs), BF16),
            pltpu.SMEM((2, LOC + 1, tiles), jnp.int32),
            pltpu.SMEM((4 * blocks,), jnp.int32),
            pltpu.SMEM((blocks,), jnp.int32),
            pltpu.SemaphoreType.DMA((6,)),
        ],
        limit=None,
    )(sat_pert[0], pert1, sat_misfit[0], misfit1, lists, lists1)
    got = [trade(values, 1) for values in sends]
    scratch = [pltpu.VMEM((8 * obs, members), BF16)]
    up, down = call(
        open_body, (shape((half, LANES), BF16), shape((full - half, LANES), BF16)), [VMEM] * 2, scratch
    )(own, got[0])
    for step, at in enumerate((1, 3, 5)):
        up, down = ring(up, 1), ring(down, -1)
        if step == 2:
            up, down, below, above = lax.optimization_barrier((up, down, below, above))
        up, down = call(
            functools.partial(step_body, at, at - CHUNKS[1][0]), (message, message), [VMEM] * 4, scratch
        )(own, got[1], up, down)
    up, down = ring(up, 1), ring(down, -1)

    anomaly, mean = call(
        background_body, (shape((members, cells), BF16), shape((1, cells), F32)), [VMEM]
    )(background[0, 0])
    result = call(
        functools.partial(final_body, 7, 7 - CHUNKS[1][0]),
        shape((members, cells), F32),
        [VMEM] * 10,
        scratch + [pltpu.VMEM((members, members), F32)],
    )(own, got[1], up, down, below, above, gram_conv, drive_conv, mean, anomaly)
    return result[None, None]


def solution(mesh):
    placed = (
        P("lat", "lon", None, None),
        P("lat", "lon", None, None),
        P("lat", "lon", None),
        P("lat", "lon", None),
        P("lat", "lon", None, None),
        P("lat", "lon", None),
        P("lat", "lon"),
        P("lat", "lon", None),
    )
    return jax.shard_map(
        shards, mesh=mesh, in_specs=placed, out_specs=P("lat", "lon", None, None), check_vma=False
    )
```

```python
import functools

import jax
import jax.numpy as jnp
from jax import lax
from jax.experimental import pallas as pl
from jax.experimental.pallas import tpu as pltpu
from jax.sharding import PartitionSpec as P

BLK = 16
LOC = 2
F32 = jnp.float32
BF16 = jnp.bfloat16
PAD = 16
LANES = 128
COLUMNS = 4
OFFSETS = (4, 3, -3, 2, -2, 1, -1, 0)
CHUNKS = ((0, 1), (1, 8))
VMEM = pltpu.VMEM
SMEM = pltpu.SMEM
LIMIT = 48 * 1024 * 1024


def call(body, outs, in_spaces, scratch=(), limit=LIMIT, flops=0, moved=0, out_space=VMEM):
    return pl.pallas_call(
        body,
        out_shape=outs,
        in_specs=[pl.BlockSpec(memory_space=space) for space in in_spaces],
        out_specs=jax.tree.map(lambda _: pl.BlockSpec(memory_space=out_space), outs),
        scratch_shapes=list(scratch),
        compiler_params=pltpu.CompilerParams(vmem_limit_bytes=limit),
        cost_estimate=pl.CostEstimate(flops=flops, bytes_accessed=moved, transcendentals=0),
    )


def transposed_dot(left, right):
    return lax.dot_general(left, right, (((0,), (0,)), ((), ())), preferred_element_type=F32)


def dot(left, right):
    return jnp.dot(left, right, preferred_element_type=F32)


def background_body(ensemble_ref, anomaly_ref, mean_ref):
    values = ensemble_ref[...].astype(F32)
    mean = jnp.mean(values, axis=0, keepdims=True)
    mean_ref[...] = mean
    anomaly_ref[...] = (values - mean).astype(BF16)


def halo_body(conv_hbm, misfit_hbm, column_hbm, halo_ref, misfit_ref, column_ref, sems):
    conv, members = conv_hbm.shape
    copies = [
        pltpu.make_async_copy(misfit_hbm, misfit_ref, sems.at[0]),
        pltpu.make_async_copy(column_hbm, column_ref, sems.at[1]),
        pltpu.make_async_copy(conv_hbm, halo_ref.at[0:conv], sems.at[2]),
    ]
    for copy in copies:
        copy.start()
    first = lax.broadcasted_iota(jnp.int32, (PAD, conv), 0) == 0
    halo_ref[conv:, :] = jnp.zeros((PAD, members), BF16)
    copies[0].wait()
    copies[1].wait()
    halo_ref[conv:, 0:conv] = jnp.where(first, misfit_ref[...].astype(F32), 0.0).astype(BF16)
    halo_ref[conv:, conv : 2 * conv] = jnp.where(first, column_ref[...].astype(F32), 0.0).astype(BF16)
    copies[2].wait()


def route_body(
    pert0_ref, pert1_ref, misfit0_ref, misfit1_ref, lists0_hbm, lists1_hbm, *refs
):
    outs = refs[: 2 * len(CHUNKS)]
    lists_ref, entry_ref, count_ref, sems = refs[2 * len(CHUNKS) :]
    tiles, obs, members = pert0_ref.shape
    blocks = count_ref.shape[0] // 2
    copies = [
        pltpu.make_async_copy(lists0_hbm, lists_ref.at[0], sems.at[0]),
        pltpu.make_async_copy(lists1_hbm, lists_ref.at[1], sems.at[1]),
    ]
    for copy in copies:
        copy.start()

    def clear(place, _):
        count_ref[place] = 0
        entry_ref[2 * place] = -1
        entry_ref[2 * place + 1] = -1
        return 0

    lax.fori_loop(0, 2 * blocks, clear, 0, unroll=True)
    for copy in copies:
        copy.wait()
    for source in range(2):
        for tile in range(tiles):
            for k in range(LOC):
                place = 2 * lists_ref[source, k, tile] + source
                used = count_ref[place]
                entry_ref[2 * place + used] = LOC * tile + k
                count_ref[place] = used + 1
    row = lax.broadcasted_iota(jnp.int32, (obs, members), 0)
    me = lax.axis_index("lon")
    planes = blocks // COLUMNS
    plane, column = me // COLUMNS, me % COLUMNS
    places = []
    for mate in range(2):
        there_column = column ^ mate
        sign = 1 - 2 * (there_column % 2)
        for at, offset in enumerate(OFFSETS):
            chunk = [at in range(low, high) for low, high in CHUNKS].index(True)
            there = (plane + sign * offset + planes) % planes
            places.append(
                (outs[mate * len(CHUNKS) + chunk], at - CHUNKS[chunk][0], there * COLUMNS + there_column)
            )
    pieces = members // LANES
    for ref, index, block in places:
        for source, pert_ref in enumerate((pert0_ref, pert1_ref)):
            for turn in range(2):
                entry = entry_ref[4 * block + 2 * source + turn]
                safe = jnp.maximum(entry, 0)
                tile = safe // LOC
                live = jnp.where(entry >= 0, lists_ref[source, LOC, tile], 0)
                factor = jnp.where(safe % LOC == 0, 1.0, 0.5**0.5).astype(F32)
                values = pert_ref[tile].astype(F32) * factor
                values = jnp.where(row < live, values, 0.0).astype(BF16)
                for part in range(pieces):
                    start = (part * 4 + 2 * source + turn) * obs
                    ref[index, start : start + obs, :] = values[:, part * LANES : (part + 1) * LANES]

    total = tiles * obs
    lane = lax.broadcasted_iota(jnp.int32, (1, total), 1)
    own_tile = lane // obs
    repeat = (
        lax.broadcasted_iota(jnp.int32, (obs, total), 1) % obs
        == lax.broadcasted_iota(jnp.int32, (obs, total), 0)
    )
    repeat = jnp.where(repeat, 1.0, 0.0).astype(BF16)
    pick = lax.broadcasted_iota(jnp.int32, (tiles, total), 1) // obs == lax.broadcasted_iota(
        jnp.int32, (tiles, total), 0
    )
    position = lax.broadcasted_iota(jnp.int32, (len(places), 1), 0)
    block = jnp.zeros((len(places), 1), jnp.int32)
    for at, (_, _, there) in enumerate(places):
        block = jnp.where(position == at, there, block)
    drive = jnp.zeros((len(places), members), F32)
    for source, (pert_ref, misfit_ref) in enumerate(
        ((pert0_ref, misfit0_ref), (pert1_ref, misfit1_ref))
    ):
        live = jnp.zeros((1, total), jnp.int32)
        named = [jnp.zeros((1, total), jnp.int32) for _ in range(LOC)]
        for tile in range(tiles):
            here = own_tile == tile
            live = jnp.where(here, lists_ref[source, LOC, tile], live)
            for k in range(LOC):
                named[k] = jnp.where(here, lists_ref[source, k, tile], named[k])
        spread = dot(misfit_ref[...], repeat)
        misfit = jnp.sum(jnp.where(pick, spread, 0.0), axis=0, keepdims=True)
        misfit = jnp.where(lane % obs < live, misfit, 0.0)
        weight = jnp.zeros((len(places), total), F32)
        for k in range(LOC):
            weight = weight + jnp.where(block == named[k], 0.5**k, 0.0)
        drive = drive + dot((weight * misfit).astype(BF16), pert_ref[...].reshape(total, members))
    upper = drive.astype(BF16).astype(F32)
    empty = jnp.zeros((PAD - 2 * pieces, LANES), F32)
    for at, (ref, index, _) in enumerate(places):
        parts = [
            piece[at : at + 1, part * LANES : (part + 1) * LANES]
            for piece in (upper, drive - upper)
            for part in range(pieces)
        ]
        ref[index, 4 * obs * pieces :, :] = jnp.concatenate(parts + [empty]).astype(BF16)


def gather_rows(own_ref, at, mate_ref, index, rows_ref):
    sources = [(own_ref, at), (mate_ref, index)]
    pieces = rows_ref.shape[1] // LANES
    count = (own_ref.shape[1] - PAD) // pieces
    drive = jnp.zeros((PAD, LANES), F32)
    for number, (ref, place) in enumerate(sources):
        for part in range(pieces):
            rows_ref[number * count : (number + 1) * count, part * LANES : (part + 1) * LANES] = ref[
                place, part * count : (part + 1) * count, :
            ]
        drive = drive + ref[place, pieces * count :, :].astype(F32)
    return drive


def triangle(size=LANES):
    across = lax.broadcasted_iota(jnp.int32, (size, size), 1)
    down = lax.broadcasted_iota(jnp.int32, (size, size), 0)
    return down, across


def packed(rows_ref, drive, right_ref=None):
    down, across = triangle()
    right_ref = rows_ref if right_ref is None else right_ref
    pieces = rows_ref.shape[1] // LANES
    bands = []
    for part in range(pieces):
        left = rows_ref[:, part * LANES : (part + 1) * LANES]
        bands.append(transposed_dot(left, right_ref[:, part * LANES :]))
    blocks, diagonals = [], []
    for part in range(0, pieces, 2):
        lower = bands[part + 1][:, 0:LANES]
        blocks.append(jnp.where(down <= across, bands[part][:, 0:LANES], lower))
        diagonals.append(jnp.sum(jnp.where(down == across, lower, 0.0), axis=0, keepdims=True))
    for part in range(pieces):
        for other in range(1, pieces - part):
            blocks.append(bands[part][:, other * LANES : (other + 1) * LANES])
    total = drive[0:pieces] + drive[pieces : 2 * pieces]
    empty = jnp.zeros((PAD - 2 * pieces - len(diagonals), LANES), F32)
    return blocks, total, jnp.concatenate(diagonals), empty


def split_drive(total, diagonals, empty):
    upper = total.astype(BF16).astype(F32)
    return jnp.concatenate([upper, total - upper, diagonals, empty]).astype(BF16)


def extra_of(extra, pieces):
    extra = extra.astype(F32)
    return extra[0:pieces] + extra[pieces : 2 * pieces], extra[2 * pieces : 2 * pieces + pieces // 2]


def open_body(own_ref, mate_ref, up_ref, down_ref, rows_ref):
    drive = gather_rows(own_ref, 0, mate_ref, 0, rows_ref)
    blocks, total, diagonals, empty = packed(rows_ref, drive)
    half = len(blocks) // 4
    for number, block in enumerate(blocks):
        ref, place = (up_ref, number) if number < half else (down_ref, number - half)
        ref[place * LANES : (place + 1) * LANES, :] = block.astype(BF16)
    down_ref[(len(blocks) - half) * LANES :, :] = split_drive(total, diagonals, empty)


def step_body(at, skip, own_ref, mate_ref, came, out, rows_ref):
    pieces = rows_ref.shape[1] // LANES
    drive = gather_rows(own_ref, at, mate_ref, at, rows_ref)
    blocks, total, diagonals, empty = packed(rows_ref, drive)
    for number, block in enumerate(blocks):
        place = (number - skip) * LANES
        if 0 <= place and place + LANES <= came.shape[0]:
            block = block + came[place : place + LANES, :].astype(F32)
        out[number * LANES : (number + 1) * LANES, :] = block.astype(BF16)
    if came.shape[0] % LANES:
        more, more_diagonals = extra_of(came[came.shape[0] - PAD :, :], pieces)
        total, diagonals = total + more, diagonals + more_diagonals
    out[len(blocks) * LANES :, :] = split_drive(total, diagonals, empty)


def conv_body(
    low_ref, halo_ref, high_ref, gram_ref, drive_ref, north_ref, south_ref, scaled_ref, spread_ref
):
    conv, members = halo_ref.shape[0] - PAD, halo_ref.shape[1]
    pieces = members // LANES
    eye = lax.broadcasted_iota(jnp.int32, (conv, conv), 0) == lax.broadcasted_iota(
        jnp.int32, (conv, conv), 1
    )
    refs = ((-1, low_ref), (0, halo_ref), (1, high_ref))
    for b, ref in refs:
        spread_ref[(b + 1) * conv : (b + 2) * conv, :] = ref[0:conv, :]
    for a, out_ref in ((-1, north_ref), (1, south_ref), (0, gram_ref)):
        drive = jnp.zeros((8, members), F32)
        for b, ref in refs:
            misfit = ref[conv : conv + 1, 0:conv]
            column = ref[conv : conv + 1, conv : 2 * conv].astype(F32)
            lat_cell = jnp.floor(column * (1.0 / BLK))
            lon_cell = column - BLK * lat_cell
            lat_place = BLK * a + lat_cell + 0.5 - 0.5 * BLK
            lon_place = BLK * b + lon_cell + 0.5 - 0.5 * BLK
            weight = jnp.exp(-(lat_place * lat_place + lon_place * lon_place) / (2.0 * BLK * BLK))
            weight = jnp.sum(jnp.where(eye, weight, 0.0), axis=1, keepdims=True)
            scaled = (weight * ref[0:conv, :].astype(F32)).astype(BF16)
            scaled_ref[(b + 1) * conv : (b + 2) * conv, :] = scaled
            drive = drive + dot(jnp.broadcast_to(misfit, (8, conv)), scaled)
        if a == 0:
            drive_ref[...] = drive[0:1]
            gram_ref[...] = transposed_dot(scaled_ref[...], spread_ref[...])
            continue
        total = jnp.concatenate(
            [drive[0:1, part * LANES : (part + 1) * LANES] for part in range(pieces)]
            + [jnp.zeros((PAD - pieces, LANES), F32)]
        )
        blocks, total, diagonals, empty = packed(scaled_ref, total, spread_ref)
        for number, block in enumerate(blocks):
            out_ref[number * LANES : (number + 1) * LANES, :] = block.astype(BF16)
        out_ref[len(blocks) * LANES :, :] = split_drive(total, diagonals, empty)


def root(system, drive):
    members = system.shape[0]
    eye = lax.broadcasted_iota(jnp.int32, system.shape, 0) == lax.broadcasted_iota(
        jnp.int32, system.shape, 1
    )
    square = jnp.sum(jnp.sum(system * system, axis=0, keepdims=True), axis=1, keepdims=True)
    inverse_scale = lax.rsqrt(square)
    power1 = system * inverse_scale
    half1 = power1.astype(BF16)
    power2 = dot(half1, half1)
    half2 = power2.astype(BF16)
    power3 = dot(half1, half2)
    power4 = dot(half2, half2)
    product = 2.25 * power1 - 1.5 * power2 + 0.25 * power3
    excess = -0.75 * (power1 + product) + 0.25 * (2.25 * power2 - 1.5 * power3 + 0.25 * power4)
    half_excess = excess.astype(BF16)
    lifted = 4.5 * excess + dot(half_excess, half_excess)
    product = 5.0625 * power1 + dot(half1, lifted.astype(BF16))
    inverse_root = 1.5 * excess - 1.125 * product - 0.5 * dot(product.astype(BF16), half_excess)
    inverse_root = inverse_root + jnp.where(eye, 3.375, 0.0)
    first = jnp.sum(inverse_root * drive, axis=1, keepdims=True)
    weight = jnp.sum(inverse_root * first, axis=0, keepdims=True) * inverse_scale
    return (jnp.sqrt((members - 1.0) * inverse_scale) * inverse_root + weight).astype(BF16)


def unpack_into(gram_ref, arrived, factors):
    pieces = gram_ref.shape[0] // LANES
    total, diagonals = 0.0, 0.0
    for ref, factor in zip(arrived, factors):
        more, more_diagonals = extra_of(ref[ref.shape[0] - PAD :, :], pieces)
        total, diagonals = total + factor * more, diagonals + factor * more_diagonals
    down, across = triangle()

    def add(part, other, block):
        place = (slice(part * LANES, (part + 1) * LANES), slice(other * LANES, (other + 1) * LANES))
        gram_ref[place] = gram_ref[place] + block

    def block_of(number):
        place = slice(number * LANES, (number + 1) * LANES)
        return sum(factor * ref[place, :].astype(F32) for ref, factor in zip(arrived, factors))

    number = 0
    for part in range(0, pieces, 2):
        block = block_of(number)
        turned = block.T
        add(part, part, jnp.where(down <= across, block, turned))
        middle = jnp.where(down == across, diagonals[number : number + 1], turned)
        add(part + 1, part + 1, jnp.where(down > across, block, middle))
        number += 1
    for part in range(pieces):
        for other in range(part + 1, pieces):
            block = block_of(number)
            add(part, other, block)
            add(other, part, block.T)
            number += 1
    return jnp.concatenate([total[part : part + 1] for part in range(pieces)], axis=1)


def base_body(
    at, own_ref, mate_ref, below_ref, above_ref, conv_ref, conv_drive_ref, gram_ref, drive_ref, rows_ref
):
    members = gram_ref.shape[0]
    pieces = members // LANES
    drive = gather_rows(own_ref, at, mate_ref, at, rows_ref)
    rows = rows_ref[...]
    eye = lax.broadcasted_iota(jnp.int32, gram_ref.shape, 0) == lax.broadcasted_iota(
        jnp.int32, gram_ref.shape, 1
    )
    gram_ref[...] = conv_ref[...] + transposed_dot(rows, rows) + jnp.where(eye, members - 1.0, 0.0)
    band = lax.axis_index("lat")
    from_below = jnp.where(band > 0, 1.0, 0.0).astype(F32)
    from_above = jnp.where(band < lax.axis_size("lat") - 1, 1.0, 0.0).astype(F32)
    total = unpack_into(gram_ref, (below_ref, above_ref), (from_below, from_above))
    own = drive[0:pieces] + drive[pieces : 2 * pieces]
    own = jnp.concatenate([own[part : part + 1] for part in range(pieces)], axis=1)
    drive_ref[...] = conv_drive_ref[...] + total + own


def final_body(up_ref, down_ref, base_ref, drive_ref, mean_ref, anomaly_ref, out_hbm, gram_ref, out_ref, sems):
    gram_ref[...] = base_ref[...]
    drive = drive_ref[...] + unpack_into(gram_ref, (up_ref, down_ref), (1.0, 1.0))
    transform = root(gram_ref[...], drive)
    members = gram_ref.shape[0]
    copies = []
    for part in range(members // LANES):
        rows = slice(part * LANES, (part + 1) * LANES)
        out_ref[rows, :] = mean_ref[...] + dot(transform[rows], anomaly_ref[...])
        copies.append(pltpu.make_async_copy(out_ref.at[rows], out_hbm.at[rows], sems.at[part]))
        copies[-1].start()
    for copy in copies:
        copy.wait()


def shards(
    background, conv_pert, conv_misfit, conv_column, sat_pert, sat_misfit, sat_rows, sat_targets
):
    members, cells = background.shape[2:]
    conv = conv_pert.shape[2]
    tiles, obs = sat_pert.shape[1:3]
    blocks, bands = lax.axis_size("lon"), lax.axis_size("lat")
    shape = jax.ShapeDtypeStruct

    pieces = members // LANES
    packet = pieces * 4 * obs + PAD
    triangles = pieces * pieces // 2
    full = triangles * LANES + PAD
    half = triangles // 4 * LANES
    message = shape((full, LANES), BF16)

    def ring(values, step):
        def target(i):
            sign = 1 - 2 * (i % 2)
            return (i + step * sign * COLUMNS) % blocks

        return lax.ppermute(values, "lon", [(i, target(i)) for i in range(blocks)])

    def trade(values, mate):
        return lax.ppermute(values, "lon", [(i, i ^ mate) for i in range(blocks)])

    halo = call(
        halo_body,
        shape((conv + PAD, members), BF16),
        [pltpu.HBM] * 3,
        [pltpu.VMEM((1, conv), BF16), pltpu.VMEM((1, conv), jnp.int32), pltpu.SemaphoreType.DMA((3,))],
        limit=None,
    )(conv_pert[0, 0], conv_misfit[0], conv_column[0])
    east = [(i, (i + 1) % blocks) for i in range(blocks)]
    west = [(target, source) for source, target in east]
    lists = jnp.concatenate([jnp.swapaxes(sat_targets[0], 0, 1), sat_rows])
    pert1, misfit1, lists1 = trade(sat_pert[0], 2), trade(sat_misfit[0], 2), trade(lists, 2)
    anomaly, mean = call(
        background_body, (shape((members, cells), BF16), shape((1, cells), F32)), [VMEM], flops=4 * members * cells, moved=4 * members * cells
    )(background[0, 0])
    halo, anomaly, mean, pert1 = lax.optimization_barrier((halo, anomaly, mean, pert1))
    counts = [high - low for low, high in CHUNKS]
    routed = call(
        route_body,
        tuple(shape((count, packet, LANES), BF16) for count in counts + counts),
        [VMEM] * 4 + [pl.ANY] * 2,
        [
            pltpu.SMEM((2, LOC + 1, tiles), jnp.int32),
            pltpu.SMEM((4 * blocks,), jnp.int32),
            pltpu.SMEM((2 * blocks,), jnp.int32),
            pltpu.SemaphoreType.DMA((2,)),
        ],
    )(sat_pert[0], pert1, sat_misfit[0], misfit1, lists, lists1)
    own, sends = routed[: len(CHUNKS)], routed[len(CHUNKS) :]
    got = [trade(values, 1) for values in sends]
    halo, _ = lax.optimization_barrier((halo, routed[-1]))
    low = lax.ppermute(halo, "lon", east)
    high = lax.ppermute(halo, "lon", west)
    def conv_halo(low, halo, high):
        gram_conv, drive_conv, to_north, to_south = call(
            conv_body,
            (shape((members, members), F32), shape((1, members), F32), message, message),
            [VMEM] * 3,
            [pltpu.VMEM((3 * conv, members), BF16), pltpu.VMEM((3 * conv, members), BF16)],
            flops=18 * conv * members * members,
            moved=8 * members * members,
        )(low, halo, high)
        return gram_conv, drive_conv, to_north, to_south

    north = [(i, (i + 1) % bands) for i in range(bands)]
    south = [(target, source) for source, target in north]
    scratch = [pltpu.VMEM((8 * obs, members), BF16)]
    step_flops, step_bytes = 16 * obs * members * members, 4 * full * LANES
    first, second = call(
        open_body, (shape((half, LANES), BF16), shape((full - half, LANES), BF16)), [VMEM] * 2, scratch
    )(own[0], got[0])
    for step in range(3):
        first = ring(first, 1)
        second = ring(second, -1)
        if step == 0:
            second, low, high = lax.optimization_barrier((second, low, high))
            gram_conv, drive_conv, to_north, to_south = conv_halo(low, halo, high)
        if step == 1:
            first, to_north, to_south = lax.optimization_barrier((first, to_north, to_south))
            below = lax.ppermute(to_north, "lat", north)
            above = lax.ppermute(to_south, "lat", south)
        if step == 2:
            first, below = lax.optimization_barrier((first, below))
            second, above = lax.optimization_barrier((second, above))
        first = call(functools.partial(step_body, 2 * step, 0), message, [VMEM] * 3, scratch, flops=step_flops, moved=step_bytes)(
            own[1], got[1], first
        )
        skip = triangles // 4 if step == 0 else 0
        second = call(functools.partial(step_body, 2 * step + 1, skip), message, [VMEM] * 3, scratch, flops=step_flops, moved=step_bytes)(
            own[1], got[1], second
        )
    first, second = ring(first, 1), ring(second, -1)

    base, drive = call(
        functools.partial(base_body, 6),
        (shape((members, members), F32), shape((1, members), F32)),
        [VMEM] * 6,
        scratch,
        flops=16 * obs * members * members,
        moved=8 * members * members,
    )(own[1], got[1], below, above, gram_conv, drive_conv)
    result = call(
        final_body,
        shape((members, cells), F32),
        [VMEM] * 6,
        [
            pltpu.VMEM((members, members), F32),
            pltpu.VMEM((members, cells), F32),
            pltpu.SemaphoreType.DMA((members // LANES,)),
        ],
        out_space=pl.ANY,
    )(first, second, base, drive, mean, anomaly)
    return result[None, None]


def solution(mesh):
    placed = (
        P("lat", "lon", None, None),
        P("lat", "lon", None, None),
        P("lat", "lon", None),
        P("lat", "lon", None),
        P("lat", "lon", None, None),
        P("lat", "lon", None),
        P("lat", "lon"),
        P("lat", "lon", None),
    )
    return jax.shard_map(
        shards, mesh=mesh, in_specs=placed, out_specs=P("lat", "lon", None, None), check_vma=False
    )
```

```python
import functools

import jax
import jax.numpy as jnp
from jax import lax
from jax.experimental import pallas as pl
from jax.experimental.pallas import tpu as pltpu
from jax.sharding import PartitionSpec as P

BLK = 16
LOC = 2
F32 = jnp.float32
BF16 = jnp.bfloat16
PAD = 16
LANES = 128
COLUMNS = 4
OFFSETS = (4, 3, -3, 2, -2, 1, -1, 0)
CHUNKS = ((0, 1), (1, 8))
VMEM = pltpu.VMEM
SMEM = pltpu.SMEM
LIMIT = 48 * 1024 * 1024


def call(body, outs, in_spaces, scratch=(), limit=LIMIT, flops=0, moved=0, out_space=VMEM):
    return pl.pallas_call(
        body,
        out_shape=outs,
        in_specs=[pl.BlockSpec(memory_space=space) for space in in_spaces],
        out_specs=jax.tree.map(lambda _: pl.BlockSpec(memory_space=out_space), outs),
        scratch_shapes=list(scratch),
        compiler_params=pltpu.CompilerParams(vmem_limit_bytes=limit),
        cost_estimate=pl.CostEstimate(flops=flops, bytes_accessed=moved, transcendentals=0),
    )


def transposed_dot(left, right):
    return lax.dot_general(left, right, (((0,), (0,)), ((), ())), preferred_element_type=F32)


def dot(left, right):
    return jnp.dot(left, right, preferred_element_type=F32)


def background_body(
    ensemble_ref, pert_ref, misfit_ref, anomaly_ref, mean_ref, kept_pert_ref, kept_misfit_ref
):
    kept_pert_ref[...] = pert_ref[...]
    kept_misfit_ref[...] = misfit_ref[...]
    values = ensemble_ref[...].astype(F32)
    mean = jnp.mean(values, axis=0, keepdims=True)
    mean_ref[...] = mean
    anomaly_ref[...] = (values - mean).astype(BF16)


def halo_body(conv_hbm, misfit_hbm, column_hbm, halo_ref, misfit_ref, column_ref, sems):
    conv, members = conv_hbm.shape
    copies = [
        pltpu.make_async_copy(misfit_hbm, misfit_ref, sems.at[0]),
        pltpu.make_async_copy(column_hbm, column_ref, sems.at[1]),
        pltpu.make_async_copy(conv_hbm, halo_ref.at[0:conv], sems.at[2]),
    ]
    for copy in copies:
        copy.start()
    first = lax.broadcasted_iota(jnp.int32, (PAD, conv), 0) == 0
    halo_ref[conv:, :] = jnp.zeros((PAD, members), BF16)
    copies[0].wait()
    copies[1].wait()
    halo_ref[conv:, 0:conv] = jnp.where(first, misfit_ref[...].astype(F32), 0.0).astype(BF16)
    halo_ref[conv:, conv : 2 * conv] = jnp.where(first, column_ref[...].astype(F32), 0.0).astype(BF16)
    copies[2].wait()


def route_body(
    pert0_ref, pert1_ref, misfit0_ref, misfit1_ref, lists0_hbm, lists1_hbm, *refs
):
    outs = refs[: 2 * len(CHUNKS)]
    lists_ref, entry_ref, count_ref, sems = refs[2 * len(CHUNKS) :]
    tiles, obs, members = pert0_ref.shape
    blocks = count_ref.shape[0] // 2
    copies = [
        pltpu.make_async_copy(lists0_hbm, lists_ref.at[0], sems.at[0]),
        pltpu.make_async_copy(lists1_hbm, lists_ref.at[1], sems.at[1]),
    ]
    for copy in copies:
        copy.start()

    def clear(place, _):
        count_ref[place] = 0
        entry_ref[2 * place] = -1
        entry_ref[2 * place + 1] = -1
        return 0

    lax.fori_loop(0, 2 * blocks, clear, 0, unroll=True)
    for copy in copies:
        copy.wait()
    for source in range(2):
        for tile in range(tiles):
            for k in range(LOC):
                place = 2 * lists_ref[source, k, tile] + source
                used = count_ref[place]
                entry_ref[2 * place + used] = LOC * tile + k
                count_ref[place] = used + 1
    row = lax.broadcasted_iota(jnp.int32, (obs, members), 0)
    me = lax.axis_index("lon")
    planes = blocks // COLUMNS
    plane, column = me // COLUMNS, me % COLUMNS
    places = []
    for mate in range(2):
        there_column = column ^ mate
        sign = 1 - 2 * (there_column % 2)
        for at, offset in enumerate(OFFSETS):
            chunk = [at in range(low, high) for low, high in CHUNKS].index(True)
            there = (plane + sign * offset + planes) % planes
            places.append(
                (outs[mate * len(CHUNKS) + chunk], at - CHUNKS[chunk][0], there * COLUMNS + there_column)
            )
    pieces = members // LANES
    for ref, index, block in places:
        for source, pert_ref in enumerate((pert0_ref, pert1_ref)):
            for turn in range(2):
                entry = entry_ref[4 * block + 2 * source + turn]
                safe = jnp.maximum(entry, 0)
                tile = safe // LOC
                live = jnp.where(entry >= 0, lists_ref[source, LOC, tile], 0)
                factor = jnp.where(safe % LOC == 0, 1.0, 0.5**0.5).astype(F32)
                values = pert_ref[tile].astype(F32) * factor
                values = jnp.where(row < live, values, 0.0).astype(BF16)
                for part in range(pieces):
                    start = (part * 4 + 2 * source + turn) * obs
                    ref[index, start : start + obs, :] = values[:, part * LANES : (part + 1) * LANES]

    total = tiles * obs
    lane = lax.broadcasted_iota(jnp.int32, (1, total), 1)
    own_tile = lane // obs
    repeat = (
        lax.broadcasted_iota(jnp.int32, (obs, total), 1) % obs
        == lax.broadcasted_iota(jnp.int32, (obs, total), 0)
    )
    repeat = jnp.where(repeat, 1.0, 0.0).astype(BF16)
    pick = lax.broadcasted_iota(jnp.int32, (tiles, total), 1) // obs == lax.broadcasted_iota(
        jnp.int32, (tiles, total), 0
    )
    position = lax.broadcasted_iota(jnp.int32, (len(places), 1), 0)
    block = jnp.zeros((len(places), 1), jnp.int32)
    for at, (_, _, there) in enumerate(places):
        block = jnp.where(position == at, there, block)
    drive = jnp.zeros((len(places), members), F32)
    for source, (pert_ref, misfit_ref) in enumerate(
        ((pert0_ref, misfit0_ref), (pert1_ref, misfit1_ref))
    ):
        live = jnp.zeros((1, total), jnp.int32)
        named = [jnp.zeros((1, total), jnp.int32) for _ in range(LOC)]
        for tile in range(tiles):
            here = own_tile == tile
            live = jnp.where(here, lists_ref[source, LOC, tile], live)
            for k in range(LOC):
                named[k] = jnp.where(here, lists_ref[source, k, tile], named[k])
        spread = dot(misfit_ref[...], repeat)
        misfit = jnp.sum(jnp.where(pick, spread, 0.0), axis=0, keepdims=True)
        misfit = jnp.where(lane % obs < live, misfit, 0.0)
        weight = jnp.zeros((len(places), total), F32)
        for k in range(LOC):
            weight = weight + jnp.where(block == named[k], 0.5**k, 0.0)
        drive = drive + dot((weight * misfit).astype(BF16), pert_ref[...].reshape(total, members))
    upper = drive.astype(BF16).astype(F32)
    empty = jnp.zeros((PAD - 2 * pieces, LANES), F32)
    for at, (ref, index, _) in enumerate(places):
        parts = [
            piece[at : at + 1, part * LANES : (part + 1) * LANES]
            for piece in (upper, drive - upper)
            for part in range(pieces)
        ]
        ref[index, 4 * obs * pieces :, :] = jnp.concatenate(parts + [empty]).astype(BF16)


def gather_rows(own_ref, at, mate_ref, index, rows_ref):
    sources = [(own_ref, at), (mate_ref, index)]
    pieces = rows_ref.shape[1] // LANES
    count = (own_ref.shape[1] - PAD) // pieces
    drive = jnp.zeros((PAD, LANES), F32)
    for number, (ref, place) in enumerate(sources):
        for part in range(pieces):
            rows_ref[number * count : (number + 1) * count, part * LANES : (part + 1) * LANES] = ref[
                place, part * count : (part + 1) * count, :
            ]
        drive = drive + ref[place, pieces * count :, :].astype(F32)
    return drive


def triangle(size=LANES):
    across = lax.broadcasted_iota(jnp.int32, (size, size), 1)
    down = lax.broadcasted_iota(jnp.int32, (size, size), 0)
    return down, across


def packed(rows_ref, drive, right_ref=None):
    down, across = triangle()
    right_ref = rows_ref if right_ref is None else right_ref
    pieces = rows_ref.shape[1] // LANES
    bands = []
    for part in range(pieces):
        left = rows_ref[:, part * LANES : (part + 1) * LANES]
        bands.append(transposed_dot(left, right_ref[:, part * LANES :]))
    blocks, diagonals = [], []
    for part in range(0, pieces, 2):
        lower = bands[part + 1][:, 0:LANES]
        blocks.append(jnp.where(down <= across, bands[part][:, 0:LANES], lower))
        diagonals.append(jnp.sum(jnp.where(down == across, lower, 0.0), axis=0, keepdims=True))
    for part in range(pieces):
        for other in range(1, pieces - part):
            blocks.append(bands[part][:, other * LANES : (other + 1) * LANES])
    total = drive[0:pieces] + drive[pieces : 2 * pieces]
    empty = jnp.zeros((PAD - 2 * pieces - len(diagonals), LANES), F32)
    return blocks, total, jnp.concatenate(diagonals), empty


def split_drive(total, diagonals, empty):
    upper = total.astype(BF16).astype(F32)
    return jnp.concatenate([upper, total - upper, diagonals, empty]).astype(BF16)


def extra_of(extra, pieces):
    extra = extra.astype(F32)
    return extra[0:pieces] + extra[pieces : 2 * pieces], extra[2 * pieces : 2 * pieces + pieces // 2]


def open_body(own_ref, mate_ref, up_ref, down_ref, rows_ref):
    drive = gather_rows(own_ref, 0, mate_ref, 0, rows_ref)
    blocks, total, diagonals, empty = packed(rows_ref, drive)
    half = len(blocks) * 1 // 2
    for number, block in enumerate(blocks):
        ref, place = (up_ref, number) if number < half else (down_ref, number - half)
        ref[place * LANES : (place + 1) * LANES, :] = block.astype(BF16)
    down_ref[(len(blocks) - half) * LANES :, :] = split_drive(total, diagonals, empty)


def step_body(at, skip, own_ref, mate_ref, came, out, rows_ref):
    pieces = rows_ref.shape[1] // LANES
    drive = gather_rows(own_ref, at, mate_ref, at, rows_ref)
    blocks, total, diagonals, empty = packed(rows_ref, drive)
    for number, block in enumerate(blocks):
        place = (number - skip) * LANES
        if 0 <= place and place + LANES <= came.shape[0]:
            block = block + came[place : place + LANES, :].astype(F32)
        out[number * LANES : (number + 1) * LANES, :] = block.astype(BF16)
    if came.shape[0] % LANES:
        more, more_diagonals = extra_of(came[came.shape[0] - PAD :, :], pieces)
        total, diagonals = total + more, diagonals + more_diagonals
    out[len(blocks) * LANES :, :] = split_drive(total, diagonals, empty)


def conv_body(
    low_ref, halo_ref, high_ref, gram_ref, drive_ref, north_ref, south_ref, scaled_ref, spread_ref
):
    conv, members = halo_ref.shape[0] - PAD, halo_ref.shape[1]
    pieces = members // LANES
    eye = lax.broadcasted_iota(jnp.int32, (conv, conv), 0) == lax.broadcasted_iota(
        jnp.int32, (conv, conv), 1
    )
    refs = ((-1, low_ref), (0, halo_ref), (1, high_ref))
    for b, ref in refs:
        spread_ref[(b + 1) * conv : (b + 2) * conv, :] = ref[0:conv, :]
    for a, out_ref in ((-1, north_ref), (1, south_ref), (0, gram_ref)):
        drive = jnp.zeros((8, members), F32)
        for b, ref in refs:
            misfit = ref[conv : conv + 1, 0:conv]
            column = ref[conv : conv + 1, conv : 2 * conv].astype(F32)
            lat_cell = jnp.floor(column * (1.0 / BLK))
            lon_cell = column - BLK * lat_cell
            lat_place = BLK * a + lat_cell + 0.5 - 0.5 * BLK
            lon_place = BLK * b + lon_cell + 0.5 - 0.5 * BLK
            weight = jnp.exp(-(lat_place * lat_place + lon_place * lon_place) / (2.0 * BLK * BLK))
            weight = jnp.sum(jnp.where(eye, weight, 0.0), axis=1, keepdims=True)
            scaled = (weight * ref[0:conv, :].astype(F32)).astype(BF16)
            scaled_ref[(b + 1) * conv : (b + 2) * conv, :] = scaled
            drive = drive + dot(jnp.broadcast_to(misfit, (8, conv)), scaled)
        if a == 0:
            drive_ref[...] = drive[0:1]
            gram_ref[...] = transposed_dot(scaled_ref[...], spread_ref[...])
            continue
        total = jnp.concatenate(
            [drive[0:1, part * LANES : (part + 1) * LANES] for part in range(pieces)]
            + [jnp.zeros((PAD - pieces, LANES), F32)]
        )
        blocks, total, diagonals, empty = packed(scaled_ref, total, spread_ref)
        for number, block in enumerate(blocks):
            out_ref[number * LANES : (number + 1) * LANES, :] = block.astype(BF16)
        out_ref[len(blocks) * LANES :, :] = split_drive(total, diagonals, empty)


def root(system, drive):
    members = system.shape[0]
    eye = lax.broadcasted_iota(jnp.int32, system.shape, 0) == lax.broadcasted_iota(
        jnp.int32, system.shape, 1
    )
    square = jnp.sum(jnp.sum(system * system, axis=0, keepdims=True), axis=1, keepdims=True)
    inverse_scale = lax.rsqrt(square)
    power1 = system * inverse_scale
    half1 = power1.astype(BF16)
    power2 = dot(half1, half1)
    half2 = power2.astype(BF16)
    power3 = dot(half1, half2)
    power4 = dot(half2, half2)
    product = 2.25 * power1 - 1.5 * power2 + 0.25 * power3
    excess = -0.75 * (power1 + product) + 0.25 * (2.25 * power2 - 1.5 * power3 + 0.25 * power4)
    half_excess = excess.astype(BF16)
    lifted = 4.5 * excess + dot(half_excess, half_excess)
    product = 5.0625 * power1 + dot(half1, lifted.astype(BF16))
    inverse_root = 1.5 * excess - 1.125 * product - 0.5 * dot(product.astype(BF16), half_excess)
    inverse_root = inverse_root + jnp.where(eye, 3.375, 0.0)
    first = jnp.sum(inverse_root * drive, axis=1, keepdims=True)
    weight = jnp.sum(inverse_root * first, axis=0, keepdims=True) * inverse_scale
    return (jnp.sqrt((members - 1.0) * inverse_scale) * inverse_root + weight).astype(BF16)


def unpack_into(gram_ref, arrived, factors):
    pieces = gram_ref.shape[0] // LANES
    total, diagonals = 0.0, 0.0
    for ref, factor in zip(arrived, factors):
        more, more_diagonals = extra_of(ref[ref.shape[0] - PAD :, :], pieces)
        total, diagonals = total + factor * more, diagonals + factor * more_diagonals
    down, across = triangle()

    def add(part, other, block):
        place = (slice(part * LANES, (part + 1) * LANES), slice(other * LANES, (other + 1) * LANES))
        gram_ref[place] = gram_ref[place] + block

    def block_of(number):
        place = slice(number * LANES, (number + 1) * LANES)
        return sum(factor * ref[place, :].astype(F32) for ref, factor in zip(arrived, factors))

    number = 0
    for part in range(0, pieces, 2):
        block = block_of(number)
        turned = block.T
        add(part, part, jnp.where(down <= across, block, turned))
        middle = jnp.where(down == across, diagonals[number : number + 1], turned)
        add(part + 1, part + 1, jnp.where(down > across, block, middle))
        number += 1
    for part in range(pieces):
        for other in range(part + 1, pieces):
            block = block_of(number)
            add(part, other, block)
            add(other, part, block.T)
            number += 1
    return jnp.concatenate([total[part : part + 1] for part in range(pieces)], axis=1)


def base_body(
    at, own_ref, mate_ref, below_ref, above_ref, conv_ref, conv_drive_ref, gram_ref, drive_ref, rows_ref
):
    members = gram_ref.shape[0]
    pieces = members // LANES
    drive = gather_rows(own_ref, at, mate_ref, at, rows_ref)
    rows = rows_ref[...]
    eye = lax.broadcasted_iota(jnp.int32, gram_ref.shape, 0) == lax.broadcasted_iota(
        jnp.int32, gram_ref.shape, 1
    )
    gram_ref[...] = conv_ref[...] + transposed_dot(rows, rows) + jnp.where(eye, members - 1.0, 0.0)
    band = lax.axis_index("lat")
    from_below = jnp.where(band > 0, 1.0, 0.0).astype(F32)
    from_above = jnp.where(band < lax.axis_size("lat") - 1, 1.0, 0.0).astype(F32)
    total = unpack_into(gram_ref, (below_ref, above_ref), (from_below, from_above))
    own = drive[0:pieces] + drive[pieces : 2 * pieces]
    own = jnp.concatenate([own[part : part + 1] for part in range(pieces)], axis=1)
    drive_ref[...] = conv_drive_ref[...] + total + own


def final_body(up_ref, down_ref, base_ref, drive_ref, mean_ref, anomaly_ref, out_hbm, gram_ref, out_ref, sems):
    gram_ref[...] = base_ref[...]
    drive = drive_ref[...] + unpack_into(gram_ref, (up_ref, down_ref), (1.0, 1.0))
    transform = root(gram_ref[...], drive)
    members = gram_ref.shape[0]
    copies = []
    for part in range(members // LANES):
        rows = slice(part * LANES, (part + 1) * LANES)
        out_ref[rows, :] = mean_ref[...] + dot(transform[rows], anomaly_ref[...])
        copies.append(pltpu.make_async_copy(out_ref.at[rows], out_hbm.at[rows], sems.at[part]))
        copies[-1].start()
    for copy in copies:
        copy.wait()


def shards(
    background, conv_pert, conv_misfit, conv_column, sat_pert, sat_misfit, sat_rows, sat_targets
):
    members, cells = background.shape[2:]
    conv = conv_pert.shape[2]
    tiles, obs = sat_pert.shape[1:3]
    blocks, bands = lax.axis_size("lon"), lax.axis_size("lat")
    shape = jax.ShapeDtypeStruct

    pieces = members // LANES
    packet = pieces * 4 * obs + PAD
    triangles = pieces * pieces // 2
    full = triangles * LANES + PAD
    half = triangles * 1 // 2 * LANES
    message = shape((full, LANES), BF16)

    def ring(values, step):
        def target(i):
            sign = 1 - 2 * (i % 2)
            return (i + step * sign * COLUMNS) % blocks

        return lax.ppermute(values, "lon", [(i, target(i)) for i in range(blocks)])

    def trade(values, mate):
        return lax.ppermute(values, "lon", [(i, i ^ mate) for i in range(blocks)])

    halo = call(
        halo_body,
        shape((conv + PAD, members), BF16),
        [pltpu.HBM] * 3,
        [pltpu.VMEM((1, conv), BF16), pltpu.VMEM((1, conv), jnp.int32), pltpu.SemaphoreType.DMA((3,))],
        limit=None,
    )(conv_pert[0, 0], conv_misfit[0], conv_column[0])
    east = [(i, (i + 1) % blocks) for i in range(blocks)]
    west = [(target, source) for source, target in east]
    lists = jnp.concatenate([jnp.swapaxes(sat_targets[0], 0, 1), sat_rows])
    pert1, misfit1, lists1 = trade(sat_pert[0], 2), trade(sat_misfit[0], 2), trade(lists, 2)
    anomaly, mean, pert0, misfit0 = call(
        background_body,
        (
            shape((members, cells), BF16),
            shape((1, cells), F32),
            shape((tiles, obs, members), BF16),
            shape((tiles, obs), BF16),
        ),
        [VMEM] * 3,
        flops=4 * members * cells,
        moved=4 * members * cells,
    )(background[0, 0], sat_pert[0], sat_misfit[0])
    halo, anomaly, mean, pert1 = lax.optimization_barrier((halo, anomaly, mean, pert1))
    counts = [high - low for low, high in CHUNKS]
    routed = call(
        route_body,
        tuple(shape((count, packet, LANES), BF16) for count in counts + counts),
        [VMEM] * 4 + [pl.ANY] * 2,
        [
            pltpu.SMEM((2, LOC + 1, tiles), jnp.int32),
            pltpu.SMEM((4 * blocks,), jnp.int32),
            pltpu.SMEM((2 * blocks,), jnp.int32),
            pltpu.SemaphoreType.DMA((2,)),
        ],
    )(pert0, pert1, misfit0, misfit1, lists, lists1)
    own, sends = routed[: len(CHUNKS)], routed[len(CHUNKS) :]
    got = [trade(values, 1) for values in sends]
    halo, _ = lax.optimization_barrier((halo, routed[-1]))
    low = lax.ppermute(halo, "lon", east)
    high = lax.ppermute(halo, "lon", west)
    def conv_halo(low, halo, high):
        gram_conv, drive_conv, to_north, to_south = call(
            conv_body,
            (shape((members, members), F32), shape((1, members), F32), message, message),
            [VMEM] * 3,
            [pltpu.VMEM((3 * conv, members), BF16), pltpu.VMEM((3 * conv, members), BF16)],
            flops=18 * conv * members * members,
            moved=8 * members * members,
        )(low, halo, high)
        return gram_conv, drive_conv, to_north, to_south

    north = [(i, (i + 1) % bands) for i in range(bands)]
    south = [(target, source) for source, target in north]
    scratch = [pltpu.VMEM((8 * obs, members), BF16)]
    step_flops, step_bytes = 16 * obs * members * members, 4 * full * LANES
    first, second = call(
        open_body, (shape((half, LANES), BF16), shape((full - half, LANES), BF16)), [VMEM] * 2, scratch
    )(own[0], got[0])
    for step in range(3):
        first = ring(first, 1)
        second = ring(second, -1)
        if step == 0:
            second, low, high = lax.optimization_barrier((second, low, high))
            gram_conv, drive_conv, to_north, to_south = conv_halo(low, halo, high)
        if step == 1:
            first, to_north, to_south = lax.optimization_barrier((first, to_north, to_south))
            below = lax.ppermute(to_north, "lat", north)
            above = lax.ppermute(to_south, "lat", south)
        if step == 2:
            second, below = lax.optimization_barrier((second, below))
        first = call(functools.partial(step_body, 2 * step, 0), message, [VMEM] * 3, scratch, flops=step_flops, moved=step_bytes)(
            own[1], got[1], first
        )
        skip = triangles * 1 // 2 if step == 0 else 0
        second = call(functools.partial(step_body, 2 * step + 1, skip), message, [VMEM] * 3, scratch, flops=step_flops, moved=step_bytes)(
            own[1], got[1], second
        )
    second, above = lax.optimization_barrier((second, above))
    first, second = ring(first, 1), ring(second, -1)

    base, drive = call(
        functools.partial(base_body, 6),
        (shape((members, members), F32), shape((1, members), F32)),
        [VMEM] * 6,
        scratch,
        flops=16 * obs * members * members,
        moved=8 * members * members,
    )(own[1], got[1], below, above, gram_conv, drive_conv)
    result = call(
        final_body,
        shape((members, cells), F32),
        [VMEM] * 6,
        [
            pltpu.VMEM((members, members), F32),
            pltpu.VMEM((members, cells), F32),
            pltpu.SemaphoreType.DMA((members // LANES,)),
        ],
        out_space=pl.ANY,
    )(first, second, base, drive, mean, anomaly)
    return result[None, None]


def solution(mesh):
    placed = (
        P("lat", "lon", None, None),
        P("lat", "lon", None, None),
        P("lat", "lon", None),
        P("lat", "lon", None),
        P("lat", "lon", None, None),
        P("lat", "lon", None),
        P("lat", "lon"),
        P("lat", "lon", None),
    )
    return jax.shard_map(
        shards, mesh=mesh, in_specs=placed, out_specs=P("lat", "lon", None, None), check_vma=False
    )
```

```python
import functools

import jax
import jax.numpy as jnp
from jax import lax
from jax.experimental import pallas as pl
from jax.experimental.pallas import tpu as pltpu
from jax.sharding import PartitionSpec as P

BLK = 16
LOC = 2
F32 = jnp.float32
BF16 = jnp.bfloat16
PAD = 16
LANES = 128
COLUMNS = 4
OFFSETS = (4, 3, -3, 2, -2, 1, -1, 0)
CHUNKS = ((0, 1), (1, 8))
VMEM = pltpu.VMEM
SMEM = pltpu.SMEM
LIMIT = 48 * 1024 * 1024


def call(body, outs, in_spaces, scratch=(), limit=LIMIT, flops=0, moved=0, out_space=VMEM):
    return pl.pallas_call(
        body,
        out_shape=outs,
        in_specs=[pl.BlockSpec(memory_space=space) for space in in_spaces],
        out_specs=jax.tree.map(lambda _: pl.BlockSpec(memory_space=out_space), outs),
        scratch_shapes=list(scratch),
        compiler_params=pltpu.CompilerParams(vmem_limit_bytes=limit),
        cost_estimate=pl.CostEstimate(flops=flops, bytes_accessed=moved, transcendentals=0),
    )


def transposed_dot(left, right):
    return lax.dot_general(left, right, (((0,), (0,)), ((), ())), preferred_element_type=F32)


def dot(left, right):
    return jnp.dot(left, right, preferred_element_type=F32)


def background_body(
    ensemble_ref, pert_ref, misfit_ref, anomaly_ref, mean_ref, kept_pert_ref, kept_misfit_ref
):
    kept_pert_ref[...] = pert_ref[...]
    kept_misfit_ref[...] = misfit_ref[...]
    values = ensemble_ref[...].astype(F32)
    mean = jnp.mean(values, axis=0, keepdims=True)
    mean_ref[...] = mean
    anomaly_ref[...] = (values - mean).astype(BF16)


def halo_body(conv_hbm, misfit_hbm, column_hbm, halo_ref, misfit_ref, column_ref, sems):
    conv, members = conv_hbm.shape
    copies = [
        pltpu.make_async_copy(misfit_hbm, misfit_ref, sems.at[0]),
        pltpu.make_async_copy(column_hbm, column_ref, sems.at[1]),
        pltpu.make_async_copy(conv_hbm, halo_ref.at[0:conv], sems.at[2]),
    ]
    for copy in copies:
        copy.start()
    first = lax.broadcasted_iota(jnp.int32, (PAD, conv), 0) == 0
    halo_ref[conv:, :] = jnp.zeros((PAD, members), BF16)
    copies[0].wait()
    copies[1].wait()
    halo_ref[conv:, 0:conv] = jnp.where(first, misfit_ref[...].astype(F32), 0.0).astype(BF16)
    halo_ref[conv:, conv : 2 * conv] = jnp.where(first, column_ref[...].astype(F32), 0.0).astype(BF16)
    copies[2].wait()


def route_body(
    pert0_ref, pert1_ref, misfit0_ref, misfit1_ref, lists0_hbm, lists1_hbm, *refs
):
    outs = refs[: 2 * len(CHUNKS)]
    lists_ref, entry_ref, count_ref, sems = refs[2 * len(CHUNKS) :]
    tiles, obs, members = pert0_ref.shape
    blocks = count_ref.shape[0] // 2
    copies = [
        pltpu.make_async_copy(lists0_hbm, lists_ref.at[0], sems.at[0]),
        pltpu.make_async_copy(lists1_hbm, lists_ref.at[1], sems.at[1]),
    ]
    for copy in copies:
        copy.start()

    def clear(place, _):
        count_ref[place] = 0
        entry_ref[2 * place] = -1
        entry_ref[2 * place + 1] = -1
        return 0

    lax.fori_loop(0, 2 * blocks, clear, 0, unroll=True)
    for copy in copies:
        copy.wait()
    for source in range(2):
        for tile in range(tiles):
            for k in range(LOC):
                place = 2 * lists_ref[source, k, tile] + source
                used = count_ref[place]
                entry_ref[2 * place + used] = LOC * tile + k
                count_ref[place] = used + 1
    row = lax.broadcasted_iota(jnp.int32, (obs, members), 0)
    me = lax.axis_index("lon")
    planes = blocks // COLUMNS
    plane, column = me // COLUMNS, me % COLUMNS
    places = []
    for mate in range(2):
        there_column = column ^ mate
        sign = 1 - 2 * (there_column % 2)
        for at, offset in enumerate(OFFSETS):
            chunk = [at in range(low, high) for low, high in CHUNKS].index(True)
            there = (plane + sign * offset + planes) % planes
            places.append(
                (outs[mate * len(CHUNKS) + chunk], at - CHUNKS[chunk][0], there * COLUMNS + there_column)
            )
    pieces = members // LANES
    for ref, index, block in places:
        for source, pert_ref in enumerate((pert0_ref, pert1_ref)):
            for turn in range(2):
                entry = entry_ref[4 * block + 2 * source + turn]
                safe = jnp.maximum(entry, 0)
                tile = safe // LOC
                live = jnp.where(entry >= 0, lists_ref[source, LOC, tile], 0)
                factor = jnp.where(safe % LOC == 0, 1.0, 0.5**0.5).astype(F32)
                values = pert_ref[tile].astype(F32) * factor
                values = jnp.where(row < live, values, 0.0).astype(BF16)
                for part in range(pieces):
                    start = (part * 4 + 2 * source + turn) * obs
                    ref[index, start : start + obs, :] = values[:, part * LANES : (part + 1) * LANES]

    total = tiles * obs
    lane = lax.broadcasted_iota(jnp.int32, (1, total), 1)
    own_tile = lane // obs
    repeat = (
        lax.broadcasted_iota(jnp.int32, (obs, total), 1) % obs
        == lax.broadcasted_iota(jnp.int32, (obs, total), 0)
    )
    repeat = jnp.where(repeat, 1.0, 0.0).astype(BF16)
    pick = lax.broadcasted_iota(jnp.int32, (tiles, total), 1) // obs == lax.broadcasted_iota(
        jnp.int32, (tiles, total), 0
    )
    position = lax.broadcasted_iota(jnp.int32, (len(places), 1), 0)
    block = jnp.zeros((len(places), 1), jnp.int32)
    for at, (_, _, there) in enumerate(places):
        block = jnp.where(position == at, there, block)
    drive = jnp.zeros((len(places), members), F32)
    for source, (pert_ref, misfit_ref) in enumerate(
        ((pert0_ref, misfit0_ref), (pert1_ref, misfit1_ref))
    ):
        live = jnp.zeros((1, total), jnp.int32)
        named = [jnp.zeros((1, total), jnp.int32) for _ in range(LOC)]
        for tile in range(tiles):
            here = own_tile == tile
            live = jnp.where(here, lists_ref[source, LOC, tile], live)
            for k in range(LOC):
                named[k] = jnp.where(here, lists_ref[source, k, tile], named[k])
        spread = dot(misfit_ref[...], repeat)
        misfit = jnp.sum(jnp.where(pick, spread, 0.0), axis=0, keepdims=True)
        misfit = jnp.where(lane % obs < live, misfit, 0.0)
        weight = jnp.zeros((len(places), total), F32)
        for k in range(LOC):
            weight = weight + jnp.where(block == named[k], 0.5**k, 0.0)
        drive = drive + dot((weight * misfit).astype(BF16), pert_ref[...].reshape(total, members))
    upper = drive.astype(BF16).astype(F32)
    empty = jnp.zeros((PAD - 2 * pieces, LANES), F32)
    for at, (ref, index, _) in enumerate(places):
        parts = [
            piece[at : at + 1, part * LANES : (part + 1) * LANES]
            for piece in (upper, drive - upper)
            for part in range(pieces)
        ]
        ref[index, 4 * obs * pieces :, :] = jnp.concatenate(parts + [empty]).astype(BF16)


def gather_rows(own_ref, at, mate_ref, index, rows_ref):
    sources = [(own_ref, at), (mate_ref, index)]
    pieces = rows_ref.shape[1] // LANES
    count = (own_ref.shape[1] - PAD) // pieces
    drive = jnp.zeros((PAD, LANES), F32)
    for number, (ref, place) in enumerate(sources):
        for part in range(pieces):
            rows_ref[number * count : (number + 1) * count, part * LANES : (part + 1) * LANES] = ref[
                place, part * count : (part + 1) * count, :
            ]
        drive = drive + ref[place, pieces * count :, :].astype(F32)
    return drive


def triangle(size=LANES):
    across = lax.broadcasted_iota(jnp.int32, (size, size), 1)
    down = lax.broadcasted_iota(jnp.int32, (size, size), 0)
    return down, across


def packed(rows_ref, drive, right_ref=None):
    down, across = triangle()
    right_ref = rows_ref if right_ref is None else right_ref
    pieces = rows_ref.shape[1] // LANES
    bands = []
    for part in range(pieces):
        left = rows_ref[:, part * LANES : (part + 1) * LANES]
        bands.append(transposed_dot(left, right_ref[:, part * LANES :]))
    blocks, diagonals = [], []
    for part in range(0, pieces, 2):
        lower = bands[part + 1][:, 0:LANES]
        blocks.append(jnp.where(down <= across, bands[part][:, 0:LANES], lower))
        diagonals.append(jnp.sum(jnp.where(down == across, lower, 0.0), axis=0, keepdims=True))
    for part in range(pieces):
        for other in range(1, pieces - part):
            blocks.append(bands[part][:, other * LANES : (other + 1) * LANES])
    total = drive[0:pieces] + drive[pieces : 2 * pieces]
    empty = jnp.zeros((PAD - 2 * pieces - len(diagonals), LANES), F32)
    return blocks, total, jnp.concatenate(diagonals), empty


def split_drive(total, diagonals, empty):
    upper = total.astype(BF16).astype(F32)
    return jnp.concatenate([upper, total - upper, diagonals, empty]).astype(BF16)


def extra_of(extra, pieces):
    extra = extra.astype(F32)
    return extra[0:pieces] + extra[pieces : 2 * pieces], extra[2 * pieces : 2 * pieces + pieces // 2]


def open_body(own_ref, mate_ref, up_ref, down_ref, rows_ref):
    drive = gather_rows(own_ref, 0, mate_ref, 0, rows_ref)
    blocks, total, diagonals, empty = packed(rows_ref, drive)
    half = len(blocks) * 1 // 2
    for number, block in enumerate(blocks):
        ref, place = (up_ref, number) if number < half else (down_ref, number - half)
        ref[place * LANES : (place + 1) * LANES, :] = block.astype(BF16)
    down_ref[(len(blocks) - half) * LANES :, :] = split_drive(total, diagonals, empty)


def step_body(at, skip, own_ref, mate_ref, came, out, rows_ref):
    pieces = rows_ref.shape[1] // LANES
    drive = gather_rows(own_ref, at, mate_ref, at, rows_ref)
    blocks, total, diagonals, empty = packed(rows_ref, drive)
    for number, block in enumerate(blocks):
        place = (number - skip) * LANES
        if 0 <= place and place + LANES <= came.shape[0]:
            block = block + came[place : place + LANES, :].astype(F32)
        out[number * LANES : (number + 1) * LANES, :] = block.astype(BF16)
    if came.shape[0] % LANES:
        more, more_diagonals = extra_of(came[came.shape[0] - PAD :, :], pieces)
        total, diagonals = total + more, diagonals + more_diagonals
    out[len(blocks) * LANES :, :] = split_drive(total, diagonals, empty)


def conv_body(
    low_ref, halo_ref, high_ref, gram_ref, drive_ref, north_ref, south_ref, scaled_ref, spread_ref
):
    conv, members = halo_ref.shape[0] - PAD, halo_ref.shape[1]
    pieces = members // LANES
    eye = lax.broadcasted_iota(jnp.int32, (conv, conv), 0) == lax.broadcasted_iota(
        jnp.int32, (conv, conv), 1
    )
    refs = ((-1, low_ref), (0, halo_ref), (1, high_ref))
    for b, ref in refs:
        spread_ref[(b + 1) * conv : (b + 2) * conv, :] = ref[0:conv, :]
    for a, out_ref in ((-1, north_ref), (1, south_ref), (0, gram_ref)):
        drive = jnp.zeros((8, members), F32)
        for b, ref in refs:
            misfit = ref[conv : conv + 1, 0:conv]
            column = ref[conv : conv + 1, conv : 2 * conv].astype(F32)
            lat_cell = jnp.floor(column * (1.0 / BLK))
            lon_cell = column - BLK * lat_cell
            lat_place = BLK * a + lat_cell + 0.5 - 0.5 * BLK
            lon_place = BLK * b + lon_cell + 0.5 - 0.5 * BLK
            weight = jnp.exp(-(lat_place * lat_place + lon_place * lon_place) / (2.0 * BLK * BLK))
            weight = jnp.sum(jnp.where(eye, weight, 0.0), axis=1, keepdims=True)
            scaled = (weight * ref[0:conv, :].astype(F32)).astype(BF16)
            scaled_ref[(b + 1) * conv : (b + 2) * conv, :] = scaled
            drive = drive + dot(jnp.broadcast_to(misfit, (8, conv)), scaled)
        if a == 0:
            drive_ref[...] = drive[0:1]
            gram_ref[...] = transposed_dot(scaled_ref[...], spread_ref[...])
            continue
        total = jnp.concatenate(
            [drive[0:1, part * LANES : (part + 1) * LANES] for part in range(pieces)]
            + [jnp.zeros((PAD - pieces, LANES), F32)]
        )
        blocks, total, diagonals, empty = packed(scaled_ref, total, spread_ref)
        for number, block in enumerate(blocks):
            out_ref[number * LANES : (number + 1) * LANES, :] = block.astype(BF16)
        out_ref[len(blocks) * LANES :, :] = split_drive(total, diagonals, empty)


def root(system, drive):
    members = system.shape[0]
    eye = lax.broadcasted_iota(jnp.int32, system.shape, 0) == lax.broadcasted_iota(
        jnp.int32, system.shape, 1
    )
    square = jnp.sum(jnp.sum(system * system, axis=0, keepdims=True), axis=1, keepdims=True)
    inverse_scale = lax.rsqrt(square)
    power1 = system * inverse_scale
    half1 = power1.astype(BF16)
    power2 = dot(half1, half1)
    half2 = power2.astype(BF16)
    power3 = dot(half1, half2)
    power4 = dot(half2, half2)
    product = 2.25 * power1 - 1.5 * power2 + 0.25 * power3
    excess = -0.75 * (power1 + product) + 0.25 * (2.25 * power2 - 1.5 * power3 + 0.25 * power4)
    half_excess = excess.astype(BF16)
    lifted = 4.5 * excess + dot(half_excess, half_excess)
    product = 5.0625 * power1 + dot(half1, lifted.astype(BF16))
    inverse_root = 1.5 * excess - 1.125 * product - 0.5 * dot(product.astype(BF16), half_excess)
    inverse_root = inverse_root + jnp.where(eye, 3.375, 0.0)
    first = jnp.sum(inverse_root * drive, axis=1, keepdims=True)
    weight = jnp.sum(inverse_root * first, axis=0, keepdims=True) * inverse_scale
    return (jnp.sqrt((members - 1.0) * inverse_scale) * inverse_root + weight).astype(BF16)


def unpack_into(gram_ref, arrived, factors):
    pieces = gram_ref.shape[0] // LANES
    total, diagonals = 0.0, 0.0
    for ref, factor in zip(arrived, factors):
        more, more_diagonals = extra_of(ref[ref.shape[0] - PAD :, :], pieces)
        total, diagonals = total + factor * more, diagonals + factor * more_diagonals
    down, across = triangle()

    def add(part, other, block):
        place = (slice(part * LANES, (part + 1) * LANES), slice(other * LANES, (other + 1) * LANES))
        gram_ref[place] = gram_ref[place] + block

    def block_of(number):
        place = slice(number * LANES, (number + 1) * LANES)
        return sum(factor * ref[place, :].astype(F32) for ref, factor in zip(arrived, factors))

    number = 0
    for part in range(0, pieces, 2):
        block = block_of(number)
        turned = block.T
        add(part, part, jnp.where(down <= across, block, turned))
        middle = jnp.where(down == across, diagonals[number : number + 1], turned)
        add(part + 1, part + 1, jnp.where(down > across, block, middle))
        number += 1
    for part in range(pieces):
        for other in range(part + 1, pieces):
            block = block_of(number)
            add(part, other, block)
            add(other, part, block.T)
            number += 1
    return jnp.concatenate([total[part : part + 1] for part in range(pieces)], axis=1)


def base_body(
    at, own_ref, mate_ref, below_ref, above_ref, conv_ref, conv_drive_ref, gram_ref, drive_ref, rows_ref
):
    members = gram_ref.shape[0]
    pieces = members // LANES
    drive = gather_rows(own_ref, at, mate_ref, at, rows_ref)
    rows = rows_ref[...]
    eye = lax.broadcasted_iota(jnp.int32, gram_ref.shape, 0) == lax.broadcasted_iota(
        jnp.int32, gram_ref.shape, 1
    )
    gram_ref[...] = conv_ref[...] + transposed_dot(rows, rows) + jnp.where(eye, members - 1.0, 0.0)
    band = lax.axis_index("lat")
    from_below = jnp.where(band > 0, 1.0, 0.0).astype(F32)
    from_above = jnp.where(band < lax.axis_size("lat") - 1, 1.0, 0.0).astype(F32)
    total = unpack_into(gram_ref, (below_ref, above_ref), (from_below, from_above))
    own = drive[0:pieces] + drive[pieces : 2 * pieces]
    own = jnp.concatenate([own[part : part + 1] for part in range(pieces)], axis=1)
    drive_ref[...] = conv_drive_ref[...] + total + own


def final_body(up_ref, down_ref, base_ref, drive_ref, mean_ref, anomaly_ref, out_hbm, gram_ref, out_ref, sems):
    gram_ref[...] = base_ref[...]
    drive = drive_ref[...] + unpack_into(gram_ref, (up_ref, down_ref), (1.0, 1.0))
    transform = root(gram_ref[...], drive)
    members = gram_ref.shape[0]
    copies = []
    for part in range(members // LANES):
        rows = slice(part * LANES, (part + 1) * LANES)
        out_ref[rows, :] = mean_ref[...] + dot(transform[rows], anomaly_ref[...])
        copies.append(pltpu.make_async_copy(out_ref.at[rows], out_hbm.at[rows], sems.at[part]))
        copies[-1].start()
    for copy in copies:
        copy.wait()


def shards(
    background, conv_pert, conv_misfit, conv_column, sat_pert, sat_misfit, sat_rows, sat_targets
):
    members, cells = background.shape[2:]
    conv = conv_pert.shape[2]
    tiles, obs = sat_pert.shape[1:3]
    blocks, bands = lax.axis_size("lon"), lax.axis_size("lat")
    shape = jax.ShapeDtypeStruct

    pieces = members // LANES
    packet = pieces * 4 * obs + PAD
    triangles = pieces * pieces // 2
    full = triangles * LANES + PAD
    half = triangles * 1 // 2 * LANES
    message = shape((full, LANES), BF16)

    def ring(values, step):
        def target(i):
            sign = 1 - 2 * (i % 2)
            return (i + step * sign * COLUMNS) % blocks

        return lax.ppermute(values, "lon", [(i, target(i)) for i in range(blocks)])

    def trade(values, mate):
        return lax.ppermute(values, "lon", [(i, i ^ mate) for i in range(blocks)])

    halo = call(
        halo_body,
        shape((conv + PAD, members), BF16),
        [pltpu.HBM] * 3,
        [pltpu.VMEM((1, conv), BF16), pltpu.VMEM((1, conv), jnp.int32), pltpu.SemaphoreType.DMA((3,))],
        limit=None,
    )(conv_pert[0, 0], conv_misfit[0], conv_column[0])
    east = [(i, (i + 1) % blocks) for i in range(blocks)]
    west = [(target, source) for source, target in east]
    lists = jnp.concatenate([jnp.swapaxes(sat_targets[0], 0, 1), sat_rows])
    pert1, misfit1, lists1 = trade(sat_pert[0], 2), trade(sat_misfit[0], 2), trade(lists, 2)
    anomaly, mean, pert0, misfit0 = call(
        background_body,
        (
            shape((members, cells), BF16),
            shape((1, cells), F32),
            shape((tiles, obs, members), BF16),
            shape((tiles, obs), BF16),
        ),
        [VMEM] * 3,
        flops=4 * members * cells,
        moved=4 * members * cells,
    )(background[0, 0], sat_pert[0], sat_misfit[0])
    halo, anomaly, mean, pert1 = lax.optimization_barrier((halo, anomaly, mean, pert1))
    counts = [high - low for low, high in CHUNKS]
    routed = call(
        route_body,
        tuple(shape((count, packet, LANES), BF16) for count in counts + counts),
        [VMEM] * 4 + [pl.ANY] * 2,
        [
            pltpu.SMEM((2, LOC + 1, tiles), jnp.int32),
            pltpu.SMEM((4 * blocks,), jnp.int32),
            pltpu.SMEM((2 * blocks,), jnp.int32),
            pltpu.SemaphoreType.DMA((2,)),
        ],
    )(pert0, pert1, misfit0, misfit1, lists, lists1)
    own, sends = routed[: len(CHUNKS)], routed[len(CHUNKS) :]
    got = [trade(values, 1) for values in sends]
    halo, _ = lax.optimization_barrier((halo, routed[-1]))
    low = lax.ppermute(halo, "lon", east)
    high = lax.ppermute(halo, "lon", west)
    def conv_halo(low, halo, high):
        gram_conv, drive_conv, to_north, to_south = call(
            conv_body,
            (shape((members, members), F32), shape((1, members), F32), message, message),
            [VMEM] * 3,
            [pltpu.VMEM((3 * conv, members), BF16), pltpu.VMEM((3 * conv, members), BF16)],
            flops=18 * conv * members * members,
            moved=8 * members * members,
        )(low, halo, high)
        return gram_conv, drive_conv, to_north, to_south

    north = [(i, (i + 1) % bands) for i in range(bands)]
    south = [(target, source) for source, target in north]
    scratch = [pltpu.VMEM((8 * obs, members), BF16)]
    step_flops, step_bytes = 16 * obs * members * members, 4 * full * LANES
    first, second = call(
        open_body, (shape((half, LANES), BF16), shape((full - half, LANES), BF16)), [VMEM] * 2, scratch
    )(own[0], got[0])
    for step in range(3):
        first = ring(first, 1)
        second = ring(second, -1)
        if step == 0:
            second, low, high = lax.optimization_barrier((second, low, high))
            gram_conv, drive_conv, to_north, to_south = conv_halo(low, halo, high)
        if step == 1:
            first, to_north, to_south = lax.optimization_barrier((first, to_north, to_south))
            below = lax.ppermute(to_north, "lat", north)
            above = lax.ppermute(to_south, "lat", south)
        if step == 2:
            second, below = lax.optimization_barrier((second, below))
        first = call(functools.partial(step_body, 2 * step, 0), message, [VMEM] * 3, scratch, flops=step_flops, moved=step_bytes)(
            own[1], got[1], first
        )
        skip = triangles * 1 // 2 if step == 0 else 0
        second = call(functools.partial(step_body, 2 * step + 1, skip), message, [VMEM] * 3, scratch, flops=step_flops, moved=step_bytes)(
            own[1], got[1], second
        )
    first, second = ring(first, 1), ring(second, -1)

    base, drive = call(
        functools.partial(base_body, 6),
        (shape((members, members), F32), shape((1, members), F32)),
        [VMEM] * 6,
        scratch,
        flops=16 * obs * members * members,
        moved=8 * members * members,
    )(own[1], got[1], below, above, gram_conv, drive_conv)
    result = call(
        final_body,
        shape((members, cells), F32),
        [VMEM] * 6,
        [
            pltpu.VMEM((members, members), F32),
            pltpu.VMEM((members, cells), F32),
            pltpu.SemaphoreType.DMA((members // LANES,)),
        ],
        out_space=pl.ANY,
    )(first, second, base, drive, mean, anomaly)
    return result[None, None]


def solution(mesh):
    placed = (
        P("lat", "lon", None, None),
        P("lat", "lon", None, None),
        P("lat", "lon", None),
        P("lat", "lon", None),
        P("lat", "lon", None, None),
        P("lat", "lon", None),
        P("lat", "lon"),
        P("lat", "lon", None),
    )
    return jax.shard_map(
        shards, mesh=mesh, in_specs=placed, out_specs=P("lat", "lon", None, None), check_vma=False
    )
```

```python
import functools

import jax
import jax.numpy as jnp
from jax import lax
from jax.experimental import pallas as pl
from jax.experimental.pallas import tpu as pltpu
from jax.sharding import PartitionSpec as P

BLK = 16
LOC = 2
F32 = jnp.float32
BF16 = jnp.bfloat16
PAD = 16
LANES = 128
COLUMNS = 4
OFFSETS = (4, 3, -3, 2, -2, 1, -1, 0)
CHUNKS = ((0, 1), (1, 8))
VMEM = pltpu.VMEM
SMEM = pltpu.SMEM
LIMIT = 48 * 1024 * 1024


def call(body, outs, in_spaces, scratch=(), limit=LIMIT, flops=0, moved=0, out_space=VMEM):
    return pl.pallas_call(
        body,
        out_shape=outs,
        in_specs=[pl.BlockSpec(memory_space=space) for space in in_spaces],
        out_specs=jax.tree.map(lambda _: pl.BlockSpec(memory_space=out_space), outs),
        scratch_shapes=list(scratch),
        compiler_params=pltpu.CompilerParams(vmem_limit_bytes=limit),
        cost_estimate=pl.CostEstimate(flops=flops, bytes_accessed=moved, transcendentals=0),
    )


def transposed_dot(left, right):
    return lax.dot_general(left, right, (((0,), (0,)), ((), ())), preferred_element_type=F32)


def dot(left, right):
    return jnp.dot(left, right, preferred_element_type=F32)


def background_body(
    ensemble_ref, pert_ref, misfit_ref, anomaly_ref, mean_ref, kept_pert_ref, kept_misfit_ref
):
    kept_pert_ref[...] = pert_ref[...]
    kept_misfit_ref[...] = misfit_ref[...]
    values = ensemble_ref[...].astype(F32)
    mean = jnp.mean(values, axis=0, keepdims=True)
    mean_ref[...] = mean
    anomaly_ref[...] = (values - mean).astype(BF16)


def halo_body(conv_hbm, misfit_hbm, column_hbm, halo_ref, misfit_ref, column_ref, sems):
    conv, members = conv_hbm.shape
    copies = [
        pltpu.make_async_copy(misfit_hbm, misfit_ref, sems.at[0]),
        pltpu.make_async_copy(column_hbm, column_ref, sems.at[1]),
        pltpu.make_async_copy(conv_hbm, halo_ref.at[0:conv], sems.at[2]),
    ]
    for copy in copies:
        copy.start()
    first = lax.broadcasted_iota(jnp.int32, (PAD, conv), 0) == 0
    halo_ref[conv:, :] = jnp.zeros((PAD, members), BF16)
    copies[0].wait()
    copies[1].wait()
    halo_ref[conv:, 0:conv] = jnp.where(first, misfit_ref[...].astype(F32), 0.0).astype(BF16)
    halo_ref[conv:, conv : 2 * conv] = jnp.where(first, column_ref[...].astype(F32), 0.0).astype(BF16)
    copies[2].wait()


def route_body(
    pert0_ref, pert1_ref, misfit0_ref, misfit1_ref, lists0_hbm, lists1_hbm, *refs
):
    outs = refs[: 2 * len(CHUNKS)]
    lists_ref, entry_ref, count_ref, sems = refs[2 * len(CHUNKS) :]
    tiles, obs, members = pert0_ref.shape
    blocks = count_ref.shape[0] // 2
    copies = [
        pltpu.make_async_copy(lists0_hbm, lists_ref.at[0], sems.at[0]),
        pltpu.make_async_copy(lists1_hbm, lists_ref.at[1], sems.at[1]),
    ]
    for copy in copies:
        copy.start()

    def clear(place, _):
        count_ref[place] = 0
        entry_ref[2 * place] = -1
        entry_ref[2 * place + 1] = -1
        return 0

    lax.fori_loop(0, 2 * blocks, clear, 0, unroll=True)
    for copy in copies:
        copy.wait()
    for source in range(2):
        for tile in range(tiles):
            for k in range(LOC):
                place = 2 * lists_ref[source, k, tile] + source
                used = count_ref[place]
                entry_ref[2 * place + used] = LOC * tile + k
                count_ref[place] = used + 1
    row = lax.broadcasted_iota(jnp.int32, (obs, members), 0)
    me = lax.axis_index("lon")
    planes = blocks // COLUMNS
    plane, column = me // COLUMNS, me % COLUMNS
    places = []
    for mate in range(2):
        there_column = column ^ mate
        sign = 1 - 2 * (there_column % 2)
        for at, offset in enumerate(OFFSETS):
            chunk = [at in range(low, high) for low, high in CHUNKS].index(True)
            there = (plane + sign * offset + planes) % planes
            places.append(
                (outs[mate * len(CHUNKS) + chunk], at - CHUNKS[chunk][0], there * COLUMNS + there_column)
            )
    pieces = members // LANES
    for ref, index, block in places:
        for source, pert_ref in enumerate((pert0_ref, pert1_ref)):
            for turn in range(2):
                entry = entry_ref[4 * block + 2 * source + turn]
                safe = jnp.maximum(entry, 0)
                tile = safe // LOC
                live = jnp.where(entry >= 0, lists_ref[source, LOC, tile], 0)
                factor = jnp.where(safe % LOC == 0, 1.0, 0.5**0.5).astype(F32)
                values = pert_ref[tile].astype(F32) * factor
                values = jnp.where(row < live, values, 0.0).astype(BF16)
                for part in range(pieces):
                    start = (part * 4 + 2 * source + turn) * obs
                    ref[index, start : start + obs, :] = values[:, part * LANES : (part + 1) * LANES]

    total = tiles * obs
    lane = lax.broadcasted_iota(jnp.int32, (1, total), 1)
    own_tile = lane // obs
    repeat = (
        lax.broadcasted_iota(jnp.int32, (obs, total), 1) % obs
        == lax.broadcasted_iota(jnp.int32, (obs, total), 0)
    )
    repeat = jnp.where(repeat, 1.0, 0.0).astype(BF16)
    pick = lax.broadcasted_iota(jnp.int32, (tiles, total), 1) // obs == lax.broadcasted_iota(
        jnp.int32, (tiles, total), 0
    )
    position = lax.broadcasted_iota(jnp.int32, (len(places), 1), 0)
    block = jnp.zeros((len(places), 1), jnp.int32)
    for at, (_, _, there) in enumerate(places):
        block = jnp.where(position == at, there, block)
    drive = jnp.zeros((len(places), members), F32)
    for source, (pert_ref, misfit_ref) in enumerate(
        ((pert0_ref, misfit0_ref), (pert1_ref, misfit1_ref))
    ):
        live = jnp.zeros((1, total), jnp.int32)
        named = [jnp.zeros((1, total), jnp.int32) for _ in range(LOC)]
        for tile in range(tiles):
            here = own_tile == tile
            live = jnp.where(here, lists_ref[source, LOC, tile], live)
            for k in range(LOC):
                named[k] = jnp.where(here, lists_ref[source, k, tile], named[k])
        spread = dot(misfit_ref[...], repeat)
        misfit = jnp.sum(jnp.where(pick, spread, 0.0), axis=0, keepdims=True)
        misfit = jnp.where(lane % obs < live, misfit, 0.0)
        weight = jnp.zeros((len(places), total), F32)
        for k in range(LOC):
            weight = weight + jnp.where(block == named[k], 0.5**k, 0.0)
        drive = drive + dot((weight * misfit).astype(BF16), pert_ref[...].reshape(total, members))
    upper = drive.astype(BF16).astype(F32)
    empty = jnp.zeros((PAD - 2 * pieces, LANES), F32)
    for at, (ref, index, _) in enumerate(places):
        parts = [
            piece[at : at + 1, part * LANES : (part + 1) * LANES]
            for piece in (upper, drive - upper)
            for part in range(pieces)
        ]
        ref[index, 4 * obs * pieces :, :] = jnp.concatenate(parts + [empty]).astype(BF16)


def gather_rows(own_ref, at, mate_ref, index, rows_ref):
    sources = [(own_ref, at), (mate_ref, index)]
    pieces = rows_ref.shape[1] // LANES
    count = (own_ref.shape[1] - PAD) // pieces
    drive = jnp.zeros((PAD, LANES), F32)
    for number, (ref, place) in enumerate(sources):
        for part in range(pieces):
            rows_ref[number * count : (number + 1) * count, part * LANES : (part + 1) * LANES] = ref[
                place, part * count : (part + 1) * count, :
            ]
        drive = drive + ref[place, pieces * count :, :].astype(F32)
    return drive


def triangle(size=LANES):
    across = lax.broadcasted_iota(jnp.int32, (size, size), 1)
    down = lax.broadcasted_iota(jnp.int32, (size, size), 0)
    return down, across


def packed(rows_ref, drive, right_ref=None):
    down, across = triangle()
    right_ref = rows_ref if right_ref is None else right_ref
    pieces = rows_ref.shape[1] // LANES
    bands = []
    for part in range(pieces):
        left = rows_ref[:, part * LANES : (part + 1) * LANES]
        bands.append(transposed_dot(left, right_ref[:, part * LANES :]))
    blocks, diagonals = [], []
    for part in range(0, pieces, 2):
        lower = bands[part + 1][:, 0:LANES]
        blocks.append(jnp.where(down <= across, bands[part][:, 0:LANES], lower))
        diagonals.append(jnp.sum(jnp.where(down == across, lower, 0.0), axis=0, keepdims=True))
    for part in range(pieces):
        for other in range(1, pieces - part):
            blocks.append(bands[part][:, other * LANES : (other + 1) * LANES])
    total = drive[0:pieces] + drive[pieces : 2 * pieces]
    empty = jnp.zeros((PAD - 2 * pieces - len(diagonals), LANES), F32)
    return blocks, total, jnp.concatenate(diagonals), empty


def split_drive(total, diagonals, empty):
    upper = total.astype(BF16).astype(F32)
    return jnp.concatenate([upper, total - upper, diagonals, empty]).astype(BF16)


def extra_of(extra, pieces):
    extra = extra.astype(F32)
    return extra[0:pieces] + extra[pieces : 2 * pieces], extra[2 * pieces : 2 * pieces + pieces // 2]


def open_body(own_ref, mate_ref, up_ref, down_ref, rows_ref):
    drive = gather_rows(own_ref, 0, mate_ref, 0, rows_ref)
    blocks, total, diagonals, empty = packed(rows_ref, drive)
    half = len(blocks) * 5 // 8
    for number, block in enumerate(blocks):
        ref, place = (up_ref, number) if number < half else (down_ref, number - half)
        ref[place * LANES : (place + 1) * LANES, :] = block.astype(BF16)
    down_ref[(len(blocks) - half) * LANES :, :] = split_drive(total, diagonals, empty)


def step_body(at, skip, own_ref, mate_ref, came, out, rows_ref):
    pieces = rows_ref.shape[1] // LANES
    drive = gather_rows(own_ref, at, mate_ref, at, rows_ref)
    blocks, total, diagonals, empty = packed(rows_ref, drive)
    for number, block in enumerate(blocks):
        place = (number - skip) * LANES
        if 0 <= place and place + LANES <= came.shape[0]:
            block = block + came[place : place + LANES, :].astype(F32)
        out[number * LANES : (number + 1) * LANES, :] = block.astype(BF16)
    if came.shape[0] % LANES:
        more, more_diagonals = extra_of(came[came.shape[0] - PAD :, :], pieces)
        total, diagonals = total + more, diagonals + more_diagonals
    out[len(blocks) * LANES :, :] = split_drive(total, diagonals, empty)


def conv_body(
    low_ref, halo_ref, high_ref, gram_ref, drive_ref, north_ref, south_ref, scaled_ref, spread_ref
):
    conv, members = halo_ref.shape[0] - PAD, halo_ref.shape[1]
    pieces = members // LANES
    eye = lax.broadcasted_iota(jnp.int32, (conv, conv), 0) == lax.broadcasted_iota(
        jnp.int32, (conv, conv), 1
    )
    refs = ((-1, low_ref), (0, halo_ref), (1, high_ref))
    for b, ref in refs:
        spread_ref[(b + 1) * conv : (b + 2) * conv, :] = ref[0:conv, :]
    for a, out_ref in ((-1, north_ref), (1, south_ref), (0, gram_ref)):
        drive = jnp.zeros((8, members), F32)
        for b, ref in refs:
            misfit = ref[conv : conv + 1, 0:conv]
            column = ref[conv : conv + 1, conv : 2 * conv].astype(F32)
            lat_cell = jnp.floor(column * (1.0 / BLK))
            lon_cell = column - BLK * lat_cell
            lat_place = BLK * a + lat_cell + 0.5 - 0.5 * BLK
            lon_place = BLK * b + lon_cell + 0.5 - 0.5 * BLK
            weight = jnp.exp(-(lat_place * lat_place + lon_place * lon_place) / (2.0 * BLK * BLK))
            weight = jnp.sum(jnp.where(eye, weight, 0.0), axis=1, keepdims=True)
            scaled = (weight * ref[0:conv, :].astype(F32)).astype(BF16)
            scaled_ref[(b + 1) * conv : (b + 2) * conv, :] = scaled
            drive = drive + dot(jnp.broadcast_to(misfit, (8, conv)), scaled)
        if a == 0:
            drive_ref[...] = drive[0:1]
            gram_ref[...] = transposed_dot(scaled_ref[...], spread_ref[...])
            continue
        total = jnp.concatenate(
            [drive[0:1, part * LANES : (part + 1) * LANES] for part in range(pieces)]
            + [jnp.zeros((PAD - pieces, LANES), F32)]
        )
        blocks, total, diagonals, empty = packed(scaled_ref, total, spread_ref)
        for number, block in enumerate(blocks):
            out_ref[number * LANES : (number + 1) * LANES, :] = block.astype(BF16)
        out_ref[len(blocks) * LANES :, :] = split_drive(total, diagonals, empty)


def root(system, drive):
    members = system.shape[0]
    eye = lax.broadcasted_iota(jnp.int32, system.shape, 0) == lax.broadcasted_iota(
        jnp.int32, system.shape, 1
    )
    square = jnp.sum(jnp.sum(system * system, axis=0, keepdims=True), axis=1, keepdims=True)
    inverse_scale = lax.rsqrt(square)
    power1 = system * inverse_scale
    half1 = power1.astype(BF16)
    power2 = dot(half1, half1)
    half2 = power2.astype(BF16)
    power3 = dot(half1, half2)
    power4 = dot(half2, half2)
    product = 2.25 * power1 - 1.5 * power2 + 0.25 * power3
    excess = -0.75 * (power1 + product) + 0.25 * (2.25 * power2 - 1.5 * power3 + 0.25 * power4)
    half_excess = excess.astype(BF16)
    lifted = 4.5 * excess + dot(half_excess, half_excess)
    product = 5.0625 * power1 + dot(half1, lifted.astype(BF16))
    inverse_root = 1.5 * excess - 1.125 * product - 0.5 * dot(product.astype(BF16), half_excess)
    inverse_root = inverse_root + jnp.where(eye, 3.375, 0.0)
    first = jnp.sum(inverse_root * drive, axis=1, keepdims=True)
    weight = jnp.sum(inverse_root * first, axis=0, keepdims=True) * inverse_scale
    return (jnp.sqrt((members - 1.0) * inverse_scale) * inverse_root + weight).astype(BF16)


def unpack_into(gram_ref, base_ref, arrived, factors):
    pieces = gram_ref.shape[0] // LANES
    total, diagonals = 0.0, 0.0
    for ref, factor in zip(arrived, factors):
        more, more_diagonals = extra_of(ref[ref.shape[0] - PAD :, :], pieces)
        total, diagonals = total + factor * more, diagonals + factor * more_diagonals
    down, across = triangle()

    def add(part, other, block):
        place = (slice(part * LANES, (part + 1) * LANES), slice(other * LANES, (other + 1) * LANES))
        gram_ref[place] = base_ref[place] + block

    def block_of(number):
        place = slice(number * LANES, (number + 1) * LANES)
        return sum(factor * ref[place, :].astype(F32) for ref, factor in zip(arrived, factors))

    number = 0
    for part in range(0, pieces, 2):
        block = block_of(number)
        turned = block.T
        add(part, part, jnp.where(down <= across, block, turned))
        middle = jnp.where(down == across, diagonals[number : number + 1], turned)
        add(part + 1, part + 1, jnp.where(down > across, block, middle))
        number += 1
    for part in range(pieces):
        for other in range(part + 1, pieces):
            block = block_of(number)
            add(part, other, block)
            add(other, part, block.T)
            number += 1
    return jnp.concatenate([total[part : part + 1] for part in range(pieces)], axis=1)


def base_body(
    at, own_ref, mate_ref, below_ref, above_ref, conv_ref, conv_drive_ref, gram_ref, drive_ref, rows_ref
):
    members = gram_ref.shape[0]
    pieces = members // LANES
    drive = gather_rows(own_ref, at, mate_ref, at, rows_ref)
    rows = rows_ref[...]
    eye = lax.broadcasted_iota(jnp.int32, gram_ref.shape, 0) == lax.broadcasted_iota(
        jnp.int32, gram_ref.shape, 1
    )
    gram_ref[...] = conv_ref[...] + transposed_dot(rows, rows) + jnp.where(eye, members - 1.0, 0.0)
    band = lax.axis_index("lat")
    from_below = jnp.where(band > 0, 1.0, 0.0).astype(F32)
    from_above = jnp.where(band < lax.axis_size("lat") - 1, 1.0, 0.0).astype(F32)
    total = unpack_into(gram_ref, gram_ref, (below_ref, above_ref), (from_below, from_above))
    own = drive[0:pieces] + drive[pieces : 2 * pieces]
    own = jnp.concatenate([own[part : part + 1] for part in range(pieces)], axis=1)
    drive_ref[...] = conv_drive_ref[...] + total + own


def final_body(up_ref, down_ref, base_ref, drive_ref, mean_ref, anomaly_ref, out_hbm, gram_ref, out_ref, sems):
    drive = drive_ref[...] + unpack_into(gram_ref, base_ref, (up_ref, down_ref), (1.0, 1.0))
    transform = root(gram_ref[...], drive)
    members = gram_ref.shape[0]
    copies = []
    for part in range(members // LANES):
        rows = slice(part * LANES, (part + 1) * LANES)
        out_ref[rows, :] = mean_ref[...] + dot(transform[rows], anomaly_ref[...])
        copies.append(pltpu.make_async_copy(out_ref.at[rows], out_hbm.at[rows], sems.at[part]))
        copies[-1].start()
    for copy in copies:
        copy.wait()


def shards(
    background, conv_pert, conv_misfit, conv_column, sat_pert, sat_misfit, sat_rows, sat_targets
):
    members, cells = background.shape[2:]
    conv = conv_pert.shape[2]
    tiles, obs = sat_pert.shape[1:3]
    blocks, bands = lax.axis_size("lon"), lax.axis_size("lat")
    shape = jax.ShapeDtypeStruct

    pieces = members // LANES
    packet = pieces * 4 * obs + PAD
    triangles = pieces * pieces // 2
    full = triangles * LANES + PAD
    half = triangles * 5 // 8 * LANES
    message = shape((full, LANES), BF16)

    def ring(values, step):
        def target(i):
            sign = 1 - 2 * (i % 2)
            return (i + step * sign * COLUMNS) % blocks

        return lax.ppermute(values, "lon", [(i, target(i)) for i in range(blocks)])

    def trade(values, mate):
        return lax.ppermute(values, "lon", [(i, i ^ mate) for i in range(blocks)])

    halo = call(
        halo_body,
        shape((conv + PAD, members), BF16),
        [pltpu.HBM] * 3,
        [pltpu.VMEM((1, conv), BF16), pltpu.VMEM((1, conv), jnp.int32), pltpu.SemaphoreType.DMA((3,))],
        limit=None,
    )(conv_pert[0, 0], conv_misfit[0], conv_column[0])
    east = [(i, (i + 1) % blocks) for i in range(blocks)]
    west = [(target, source) for source, target in east]
    lists = jnp.concatenate([jnp.swapaxes(sat_targets[0], 0, 1), sat_rows])
    pert1, misfit1, lists1 = trade(sat_pert[0], 2), trade(sat_misfit[0], 2), trade(lists, 2)
    anomaly, mean, pert0, misfit0 = call(
        background_body,
        (
            shape((members, cells), BF16),
            shape((1, cells), F32),
            shape((tiles, obs, members), BF16),
            shape((tiles, obs), BF16),
        ),
        [VMEM] * 3,
        flops=4 * members * cells,
        moved=4 * members * cells,
    )(background[0, 0], sat_pert[0], sat_misfit[0])
    halo, anomaly, mean, pert1 = lax.optimization_barrier((halo, anomaly, mean, pert1))
    counts = [high - low for low, high in CHUNKS]
    routed = call(
        route_body,
        tuple(shape((count, packet, LANES), BF16) for count in counts + counts),
        [VMEM] * 4 + [pl.ANY] * 2,
        [
            pltpu.SMEM((2, LOC + 1, tiles), jnp.int32),
            pltpu.SMEM((4 * blocks,), jnp.int32),
            pltpu.SMEM((2 * blocks,), jnp.int32),
            pltpu.SemaphoreType.DMA((2,)),
        ],
    )(pert0, pert1, misfit0, misfit1, lists, lists1)
    own, sends = routed[: len(CHUNKS)], routed[len(CHUNKS) :]
    got = [trade(values, 1) for values in sends]
    halo, _ = lax.optimization_barrier((halo, routed[-1]))
    low = lax.ppermute(halo, "lon", east)
    high = lax.ppermute(halo, "lon", west)
    def conv_halo(low, halo, high):
        gram_conv, drive_conv, to_north, to_south = call(
            conv_body,
            (shape((members, members), F32), shape((1, members), F32), message, message),
            [VMEM] * 3,
            [pltpu.VMEM((3 * conv, members), BF16), pltpu.VMEM((3 * conv, members), BF16)],
            flops=18 * conv * members * members,
            moved=8 * members * members,
        )(low, halo, high)
        return gram_conv, drive_conv, to_north, to_south

    north = [(i, (i + 1) % bands) for i in range(bands)]
    south = [(target, source) for source, target in north]
    scratch = [pltpu.VMEM((8 * obs, members), BF16)]
    step_flops, step_bytes = 16 * obs * members * members, 4 * full * LANES
    first, second = call(
        open_body, (shape((half, LANES), BF16), shape((full - half, LANES), BF16)), [VMEM] * 2, scratch
    )(own[0], got[0])
    for step in range(3):
        first = ring(first, 1)
        second = ring(second, -1)
        if step == 0:
            second, low, high = lax.optimization_barrier((second, low, high))
            gram_conv, drive_conv, to_north, to_south = conv_halo(low, halo, high)
        if step == 1:
            first, to_north, to_south = lax.optimization_barrier((first, to_north, to_south))
            below = lax.ppermute(to_north, "lat", north)
            above = lax.ppermute(to_south, "lat", south)
        if step == 2:
            second, below = lax.optimization_barrier((second, below))
        first = call(functools.partial(step_body, 2 * step, 0), message, [VMEM] * 3, scratch, flops=step_flops, moved=step_bytes)(
            own[1], got[1], first
        )
        skip = triangles * 5 // 8 if step == 0 else 0
        second = call(functools.partial(step_body, 2 * step + 1, skip), message, [VMEM] * 3, scratch, flops=step_flops, moved=step_bytes)(
            own[1], got[1], second
        )
    first, second = ring(first, 1), ring(second, -1)

    base, drive = call(
        functools.partial(base_body, 6),
        (shape((members, members), F32), shape((1, members), F32)),
        [VMEM] * 6,
        scratch,
        flops=16 * obs * members * members,
        moved=8 * members * members,
    )(own[1], got[1], below, above, gram_conv, drive_conv)
    result = call(
        final_body,
        shape((members, cells), F32),
        [VMEM] * 6,
        [
            pltpu.VMEM((members, members), F32),
            pltpu.VMEM((members, cells), F32),
            pltpu.SemaphoreType.DMA((members // LANES,)),
        ],
        out_space=pl.ANY,
    )(first, second, base, drive, mean, anomaly)
    return result[None, None]


def solution(mesh):
    placed = (
        P("lat", "lon", None, None),
        P("lat", "lon", None, None),
        P("lat", "lon", None),
        P("lat", "lon", None),
        P("lat", "lon", None, None),
        P("lat", "lon", None),
        P("lat", "lon"),
        P("lat", "lon", None),
    )
    return jax.shard_map(
        shards, mesh=mesh, in_specs=placed, out_specs=P("lat", "lon", None, None), check_vma=False
    )
```
